32 devices in a mesh: tok: 8 (over y, x, core), mdl: 4 (over z).
Axes of the slice: x: 2, y: 2, z: 4, core: 2. Of those that a mesh axis runs over, the one named last changes fastest.
Arguments:
- hidden: bfloat16 [4096, 2048], P('tok'), may hold values from -40 to 40
- segment_ids: int32 [4096], replicated, may hold values from 0 to 3, never falling along the last dimension, each value on 1 to 2048 neighbouring positions
- routes: int32 [4096, 2], P('tok'), may hold values from 0 to 7, all different within a row; in each aligned block of 512 rows (0 to 511, 512 to 1023, ...) at most 256 rows name the same one
- norm_gain: float32 [2048], replicated, may hold values from 0.5 to 1.5
- router_weight: float32 [2048, 8], replicated, may hold values from -0.125 to 0.125
- query_weight: bfloat16 [8, 2048, 2048], P(None, 'tok', 'mdl'), may hold values from -2 to 2
- kv_weight: bfloat16 [2, 2048, 2048], P(None, 'tok', 'mdl'), may hold values from -16 to 16
- out_weight: bfloat16 [8, 2048, 2048], P(None, 'mdl', 'tok'), may hold values from -0.5 to 0.5
- page_table: int32 [256], P('tok'), may hold values from 0 to 255, as said below
Outputs:
- output: bfloat16 [4096, 2048], P('tok', 'mdl')
- cache: bfloat16 [256, 16, 2, 2048], P('tok', None, None, 'mdl')
The draws below stay inside these ranges and needn't reach their ends.
Inputs may be any that keep to these rules, and one draw needn't show every extreme that they name: `segment_ids`: Non-decreasing along the tokens; every prompt number 0 to 3 occurs, each prompt 1 to 2048 tokens long, one exactly 2048. `routes`: each token names 2 different experts; among the 512 tokens of an aligned block no expert is named more than 256 times, and some block reaches 256. `page_table`: A permutation of the 256 physical pages; of the 32 logical pages of each aligned block, exactly 4 lie in each aligned range of 32 physical pages.
All inputs are finite; a program needn't handle non-finite values.
Results may differ from the reference program's by a relative error of at most 0.019.
Values may be sent and summed in bfloat16 or wider, within the bound.
A program may use at most 128 MiB of HBM per device.

```python
import math
import jax
import jax.numpy as jnp
import numpy as np
from jax import lax

D = 2048
HEADS = 16
HDIM = 128
AEXP = 8
ATOP = 2
PAGE = 16
SEGS = 4
TOK_DEV = 512
TOKENS = 4096
MOST_LEN = 2048
CAP = 256
PG_DEV = 32
PAGES = 256
SHARDS = 8
N_MDL = 4


def loguniform_draw(key, shape, lowest, highest):
    return jnp.exp(jax.random.uniform(key, shape, jnp.float32, math.log(lowest), math.log(highest)))


def clipped_normal(key, shape, bound_value):
    return jnp.clip(jax.random.normal(key, shape, jnp.float32), -bound_value, bound_value)


def draw_hidden(key, part):
    columns = loguniform_draw(jax.random.fold_in(key, 1), (D,), 0.3, 3.0)
    base = clipped_normal(jax.random.fold_in(key, 2), (TOKENS, D), 6.0)
    values = base * columns[None, :]
    return values.astype(jnp.bfloat16)


def attention_weights(key):
    factor = 2.0 / math.sqrt(D)
    queries = clipped_normal(jax.random.fold_in(key, 21), (AEXP, D, HEADS * HDIM), 5.0) * factor
    keys = clipped_normal(jax.random.fold_in(key, 22), (D, HEADS * HDIM), 5.0) * factor
    values = clipped_normal(jax.random.fold_in(key, 23), (D, HEADS * HDIM), 5.0) / math.sqrt(D)
    return (queries, jnp.stack([keys, values]))


def draw_query_weight(key, part):
    return attention_weights(key)[0].astype(jnp.bfloat16)


def draw_kv_weight(key, part):
    return attention_weights(key)[1].astype(jnp.bfloat16)


def one_permutation(subkey):
    return jax.random.permutation(subkey, PG_DEV)


def draw_page_table(key, part):
    per_peer = PG_DEV // SHARDS
    source_ranks = jax.vmap(one_permutation)(jax.random.split(jax.random.fold_in(key, 31), SHARDS))
    target_orders = jax.vmap(one_permutation)(jax.random.split(jax.random.fold_in(key, 32), SHARDS))
    targets = source_ranks // per_peer
    within = source_ranks % per_peer
    sources = jnp.arange(SHARDS, dtype=jnp.int32)[:, None]
    local_page = target_orders[targets, sources * per_peer + within]
    return (targets * PG_DEV + local_page).reshape(PAGES).astype(jnp.int32)


def steps_of(stream_key, extent, cuts, smallest, top_value):
    gain, own = 1.0, jax.random.fold_in(stream_key, 6)
    for axis_at, shards_of in cuts:
        heights = jnp.exp(jax.random.uniform(jax.random.fold_in(own, axis_at), (shards_of,), jnp.float32, smallest / len(cuts), top_value / len(cuts)))
        gain = gain * jnp.repeat(heights, extent[axis_at] // shards_of).reshape([-1 if axis == axis_at else 1 for axis in range(len(extent))])
    return gain


def length_profile(amount, total, limit, lean):
    portions = [(1 << 20) // math.isqrt(rank ** lean) + 1 for rank in range(2, amount + 1)]
    surplus, given = total - limit - (amount - 1), [1] * (amount - 1)
    while surplus > 0:
        free = [i for i in range(amount - 1) if given[i] < limit]
        mass, budget = sum([portions[i] for i in free]), surplus
        for i in free:
            addition = min(limit - given[i], max(1, budget * portions[i] // mass), surplus)
            given[i] = given[i] + addition
            surplus = surplus - addition
    return np.array([limit] + given)


def ragged_sizes(stream_key, amount, total, most, lean):
    if amount == 2:
        one = jax.random.randint(stream_key, (), max(1, total - most), min(most, total - 1) + 1)
        return jnp.stack([one, total - one])
    sizes = jnp.asarray(length_profile(amount, total, most, lean), jnp.int32)
    pairs = (amount - 1) // 2
    giver, receiver = sizes[1:1 + 2 * pairs:2], sizes[2:2 + 2 * pairs:2]
    room = jnp.minimum(giver - 1, most - receiver)
    passed = jax.random.randint(jax.random.fold_in(stream_key, 1), (pairs,), 0, 1 << 20) % (room + 1)
    sizes = sizes.at[1:1 + 2 * pairs:2].set(giver - passed).at[2:2 + 2 * pairs:2].set(receiver + passed)
    return sizes[jax.random.permutation(jax.random.fold_in(stream_key, 2), amount)]


def deal_out(stream_key, own, number, rows, number_of, top, bound, slope):
    order = jax.random.permutation(stream_key, number_of)
    heavy_load, common = shares(number_of, rows * top, bound, slope, True), shares(number_of, rows * top, bound, slope, False)
    places = jnp.arange(number_of)

    def named(sizes, turn):
        used = int((sizes > 0).sum())
        fixed = max(1, used // 4)
        shifted = fixed + (places - fixed + turn * (used - fixed)) % max(1, number_of - fixed)
        return jnp.zeros((number_of,), jnp.int32).at[order[jnp.where(places < fixed, places, shifted)]].set(jnp.asarray(sizes, jnp.int32))

    sizes = jnp.where(number % 4 == 0, named(heavy_load, number // 4), named(common, number - number // 4 - 1))
    mixed = jax.random.permutation(jax.random.fold_in(own, 3), number_of)
    giver, receiver = mixed[0:number_of // 2 * 2:2], mixed[1:number_of // 2 * 2:2]
    margin = jnp.minimum(sizes[giver] - 1, bound - sizes[receiver]) // 2
    margin = jnp.where((giver == order[0]) | (receiver == order[0]) | (sizes[receiver] == 0), 0, jnp.maximum(margin, 0))
    shifted = jax.random.randint(jax.random.fold_in(own, 4), (number_of // 2,), 0, 1 << 20) % (margin + 1)
    sizes = sizes.at[giver].add(-shifted).at[receiver].add(shifted)
    members = jnp.searchsorted(jnp.cumsum(sizes), jnp.arange(rows * top), side="right").astype(jnp.int32)
    listing = members.reshape(top, rows).T
    listing = listing[jax.random.permutation(jax.random.fold_in(own, 1), rows)]
    turn = jax.random.randint(jax.random.fold_in(own, 2), (rows, 1), 0, top)
    return jnp.take_along_axis(listing, (jnp.arange(top)[None, :] + turn) % top, axis=1)


def shares(number_of, total, bound, skew, full):
    portions = [(1 << 20) // math.isqrt(standing ** skew) + 1 for standing in range(1, number_of + 1)]
    largest = bound if full else min(bound, max(-(-total // number_of), total * portions[0] // sum(portions)))
    least = 1 if total - largest >= number_of - 1 else 0
    holding, surplus = [largest] + [least] * (number_of - 1), total - largest - least * (number_of - 1)
    while surplus > 0:
        candidates = [i for i in range(1, number_of) if holding[i] < largest] or [i for i in range(1, number_of) if holding[i] < bound]
        mass, budget = sum([portions[i] for i in candidates]), surplus
        for i in candidates:
            more = min(bound - holding[i], max(1, budget * portions[i] // mass), surplus)
            holding[i] = holding[i] + more
            surplus = surplus - more
    return np.array(holding)


def noise(key, extent, width, bound, cuts=(), kind=jnp.bfloat16):
    drawn = width * jax.random.normal(key, extent, jnp.float32)
    if cuts:
        drawn = drawn * steps_of(key, extent, cuts, -0.22, 0.18)
    return jnp.clip(drawn, -bound, bound).astype(kind)


def setup_inputs(seed: int = 0) -> dict:
    seeds = jax.random.split(jax.random.key(seed), 10)
    hidden = draw_hidden(jax.random.fold_in(seeds[9], 71), 0)
    segment_ids = jnp.searchsorted(jnp.cumsum(ragged_sizes(seeds[1], SEGS, TOKENS, MOST_LEN, 2)), jnp.arange(TOKENS), side="right").astype(jnp.int32)
    routes_keys = jax.random.split(jax.random.fold_in(seeds[2], 1), TOKENS // TOK_DEV)
    routes_turns = jax.random.permutation(jax.random.fold_in(seeds[2], 3), TOKENS // TOK_DEV)
    routes = jax.vmap(lambda own, number: deal_out(jax.random.fold_in(seeds[2], 2), own, number, TOK_DEV, AEXP, ATOP, CAP, 1))(routes_keys, routes_turns).reshape((TOKENS, ATOP))
    norm_gain = jnp.clip(1.0 + 0.1 * jax.random.normal(seeds[3], (D,), jnp.float32), 0.5, 1.5)
    router_weight = noise(seeds[4], (D, AEXP), D ** -0.5, 0.125, (), jnp.float32)
    query_weight = draw_query_weight(jax.random.fold_in(seeds[9], 71), 0)
    kv_weight = draw_kv_weight(jax.random.fold_in(seeds[9], 71), 0)
    out_weight = noise(seeds[7], (AEXP, HEADS * HDIM, D), (HEADS * HDIM // 16) ** -0.5, 0.5, ((1, 4), (2, 8)))
    page_table = draw_page_table(jax.random.fold_in(seeds[9], 71), 0)
    return dict(hidden=hidden, segment_ids=segment_ids, routes=routes, norm_gain=norm_gain, router_weight=router_weight, query_weight=query_weight, kv_weight=kv_weight, out_weight=out_weight, page_table=page_table)


EPSILON = 1e-05
MASKED = -1e+30

def rms_norm(hidden, norm_gain):
    values = hidden.astype(jnp.float32)
    factor = lax.rsqrt(lax.optimization_barrier(jnp.mean(values * values, axis=-1, keepdims=True)) + EPSILON)
    return (values * factor * norm_gain).astype(jnp.bfloat16)

def route_gates(normed, router_weight, routes):
    logits = jnp.dot(normed.astype(jnp.float32), router_weight, precision=lax.Precision.HIGHEST)
    expert_ids = jnp.arange(logits.shape[1], dtype=jnp.int32)
    picked = routes[:, :, None] == expert_ids[None, None, :]
    chosen = lax.optimization_barrier(jnp.sum(jnp.where(picked, logits[:, None, :], jnp.float32(0.0)), axis=-1))
    return jax.nn.softmax(chosen, axis=-1)

def reference(hidden, segment_ids, routes, norm_gain, router_weight, query_weight, kv_weight, out_weight, page_table):
    head_cols = HEADS * HDIM
    normed = rms_norm(hidden, norm_gain)
    gates = route_gates(normed, router_weight, routes)
    key_values = jnp.stack([jnp.dot(normed, kv_weight[0], preferred_element_type=jnp.float32), jnp.dot(normed, kv_weight[1], preferred_element_type=jnp.float32)], axis=1).astype(jnp.bfloat16)

    def expert_queries(carry, expert):
        projected = jnp.dot(normed, query_weight[expert], preferred_element_type=jnp.float32).astype(jnp.bfloat16)
        return (jnp.where((routes == expert)[:, :, None], projected[:, None, :], carry), None)
    queries, _ = lax.scan(expert_queries, jnp.zeros((TOKENS, ATOP, head_cols), jnp.bfloat16), jnp.arange(AEXP, dtype=jnp.int32))
    query_block = math.gcd(TOKENS, 1024)
    window = min(TOKENS, MOST_LEN + query_block)
    blocks = TOKENS // query_block
    by_head_q = queries.reshape(TOKENS, ATOP, HEADS, HDIM).transpose(2, 1, 0, 3)
    by_head_k = key_values[:, 0].reshape(TOKENS, HEADS, HDIM).transpose(1, 0, 2)
    by_head_v = key_values[:, 1].reshape(TOKENS, HEADS, HDIM).transpose(1, 0, 2)
    zero_index = jnp.zeros((), jnp.int32)

    def attend(index):
        head = (index // blocks).astype(jnp.int32)
        first = (index % blocks * query_block).astype(jnp.int32)
        key_first = jnp.clip(first + query_block - window, 0, TOKENS - window).astype(jnp.int32)
        q_rows = lax.dynamic_slice(by_head_q, (head, zero_index, first, zero_index), (1, ATOP, query_block, HDIM))[0].astype(jnp.float32)
        k_rows = lax.dynamic_slice(by_head_k, (head, key_first, zero_index), (1, window, HDIM))[0].astype(jnp.float32)
        v_rows = lax.dynamic_slice(by_head_v, (head, key_first, zero_index), (1, window, HDIM))[0].astype(jnp.float32)
        q_seg = lax.dynamic_slice(segment_ids, (first,), (query_block,))
        k_seg = lax.dynamic_slice(segment_ids, (key_first,), (window,))
        q_pos = first + jnp.arange(query_block, dtype=jnp.int32)
        k_pos = key_first + jnp.arange(window, dtype=jnp.int32)
        allowed = (q_seg[:, None] == k_seg[None, :]) & (k_pos[None, :] <= q_pos[:, None])
        scores = jnp.einsum('sqd,kd->sqk', q_rows, k_rows) / math.sqrt(HDIM)
        scores = jnp.where(allowed[None], scores, jnp.float32(MASKED))
        peak = lax.optimization_barrier(jnp.max(scores, axis=-1, keepdims=True))
        expon = jnp.where(allowed[None], jnp.exp(scores - peak), jnp.float32(0.0))
        totals = lax.optimization_barrier(jnp.sum(expon, axis=-1, keepdims=True))
        probs = expon.astype(jnp.bfloat16).astype(jnp.float32)
        return (jnp.einsum('sqk,kd->sqd', probs, v_rows) / totals).astype(jnp.bfloat16)
    attended = lax.map(attend, jnp.arange(HEADS * blocks, dtype=jnp.int32))
    attended = attended.reshape(HEADS, blocks, ATOP, query_block, HDIM).transpose(1, 3, 2, 0, 4).reshape(TOKENS, ATOP, head_cols)
    group_cols = head_cols // N_MDL

    def group_output(total, group):
        col_first = (group * group_cols).astype(jnp.int32)
        group_rows = lax.dynamic_slice_in_dim(attended, col_first, group_cols, 2)

        def expert_output(partial_value, expert):
            chosen = routes == expert
            rows = lax.optimization_barrier(jnp.sum(jnp.where(chosen[:, :, None], group_rows.astype(jnp.float32), jnp.float32(0.0)), axis=1)).astype(jnp.bfloat16)
            weight = lax.optimization_barrier(jnp.sum(jnp.where(chosen, gates, jnp.float32(0.0)), axis=1))
            block = lax.dynamic_slice_in_dim(out_weight[expert], col_first, group_cols, 0)
            return (partial_value + weight[:, None] * jnp.dot(rows, block, preferred_element_type=jnp.float32), None)
        partial_value, _ = lax.scan(expert_output, jnp.zeros((TOKENS, D), jnp.float32), jnp.arange(AEXP, dtype=jnp.int32))
        rounded = lax.optimization_barrier(partial_value.astype(jnp.bfloat16))
        return (total + rounded.astype(jnp.float32), None)
    mixed, _ = lax.scan(group_output, jnp.zeros((TOKENS, D), jnp.float32), jnp.arange(N_MDL, dtype=jnp.int32))
    output = (hidden.astype(jnp.float32) + mixed).astype(jnp.bfloat16)
    logical = key_values.reshape(PAGES, PAGE, 2, head_cols)
    cache = jnp.zeros_like(logical).at[page_table].set(logical)
    return (output, cache)
```

```python
import functools
import math

import jax
import jax.numpy as jnp
from jax import lax
from jax.experimental import pallas as pl
from jax.experimental.pallas import tpu as pltpu
from jax.sharding import PartitionSpec as P

HDIM = 128
SEGS = 4
EPSILON = 1e-05
MASKED = -1e30
VMEM_BYTES = 48 * 1024 * 1024
SCALE = math.log2(math.e) / math.sqrt(HDIM)


def rms_norm(hidden, norm_gain):
    values = hidden.astype(jnp.float32)
    factor = lax.rsqrt(jnp.mean(values * values, axis=-1, keepdims=True) + EPSILON)
    return (values * factor * norm_gain).astype(jnp.bfloat16)


def route_gates(normed, router_weight, routes):
    logits = jnp.dot(normed.astype(jnp.float32), router_weight, precision=lax.Precision.HIGHEST)
    expert_ids = jnp.arange(logits.shape[1], dtype=jnp.int32)
    picked = routes[:, :, None] == expert_ids[None, None, :]
    chosen = jnp.sum(jnp.where(picked, logits[:, None, :], jnp.float32(0.0)), axis=-1)
    gates = jax.nn.softmax(chosen, axis=-1)
    return jnp.sum(jnp.where(picked, gates[:, :, None], jnp.float32(0.0)), axis=1)


def params():
    return pltpu.CompilerParams(
        dimension_semantics=("arbitrary",), vmem_limit_bytes=VMEM_BYTES
    )


def kv_kernel(x_ref, w_ref, out_ref):
    depth = w_ref.shape[0] * w_ref.shape[2]
    w = w_ref[:, 0].reshape(depth, w_ref.shape[3])
    out_ref[0] = jnp.dot(x_ref[...], w, preferred_element_type=jnp.float32).astype(jnp.bfloat16)


def project_kv(normed, weight):
    shards, kinds, rows, cols = weight.shape
    tokens, width = normed.shape
    return pl.pallas_call(
        kv_kernel,
        grid=(kinds,),
        in_specs=[
            pl.BlockSpec((tokens, width), lambda c: (0, 0)),
            pl.BlockSpec((shards, 1, rows, cols), lambda c: (0, c, 0, 0)),
        ],
        out_specs=pl.BlockSpec((1, tokens, cols), lambda c: (c, 0, 0)),
        out_shape=jax.ShapeDtypeStruct((kinds, tokens, cols), jnp.bfloat16),
        compiler_params=params(),
        cost_estimate=pl.CostEstimate(
            flops=2 * kinds * tokens * width * cols,
            bytes_accessed=2 * (weight.size + normed.size + kinds * tokens * cols),
            transcendentals=0,
        ),
        name="project_kv",
    )(normed, weight)


def query_kernel(x_ref, routes_ref, w_ref, out_ref):
    expert = pl.program_id(0)
    depth = w_ref.shape[0] * w_ref.shape[2]
    w = w_ref[:, 0].reshape(depth, w_ref.shape[3])
    y = jnp.dot(x_ref[...], w, preferred_element_type=jnp.float32).astype(jnp.bfloat16)

    @pl.when(expert == 0)
    def _():
        out_ref[...] = jnp.zeros_like(out_ref)

    for slot in range(out_ref.shape[0]):
        mine = routes_ref[:, slot : slot + 1] == expert
        out_ref[slot] = jnp.where(mine, y, out_ref[slot])


def project_queries(normed, routes, weight):
    shards, experts, rows, cols = weight.shape
    tokens, width = normed.shape
    slots = routes.shape[1]
    return pl.pallas_call(
        query_kernel,
        grid=(experts,),
        in_specs=[
            pl.BlockSpec((tokens, width), lambda e: (0, 0)),
            pl.BlockSpec((tokens, slots), lambda e: (0, 0)),
            pl.BlockSpec((shards, 1, rows, cols), lambda e: (0, e, 0, 0)),
        ],
        out_specs=pl.BlockSpec((slots, tokens, cols), lambda e: (0, 0, 0)),
        out_shape=jax.ShapeDtypeStruct((slots, tokens, cols), jnp.bfloat16),
        compiler_params=params(),
        cost_estimate=pl.CostEstimate(
            flops=2 * experts * tokens * width * cols,
            bytes_accessed=2 * (weight.size + normed.size + slots * tokens * cols),
            transcendentals=0,
        ),
        name="project_queries",
    )(normed, routes, weight)


def attention_kernel(bounds_ref, q_ref, lower_ref, kv_ref, out_ref, *, block_k, heads, tile):
    pos_first = bounds_ref[0]
    step = pl.program_id(1)
    first = pos_first + step * tile
    low = bounds_ref[1 + 2 * step]
    high = bounds_ref[2 + 2 * step]
    slots = q_ref.shape[0]
    columns = slots * tile
    per_shard = kv_ref.shape[2] // block_k
    begin = low // block_k
    end = (first + tile - 1) // block_k + 1
    q_pos = first + lax.broadcasted_iota(jnp.int32, (1, columns), 1) % tile
    lower = jnp.concatenate([lower_ref[0]] * slots, axis=1)
    queries = [
        q_ref[:, :, h * HDIM : (h + 1) * HDIM].reshape(columns, HDIM) for h in range(heads)
    ]

    def body(block, carry, masked):
        shard = block // per_shard
        rows = pl.ds((block % per_shard) * block_k, block_k)
        if masked:
            k_pos = block * block_k + lax.broadcasted_iota(jnp.int32, (block_k, columns), 0)
            allowed = (k_pos >= lower) & (k_pos <= q_pos)
        result = []
        for h in range(heads):
            peak, total, accum = carry[h]
            span = slice(h * HDIM, (h + 1) * HDIM)
            keys = kv_ref[shard, 0, rows, span]
            values = kv_ref[shard, 1, rows, span]
            scores = lax.dot_general(
                keys, queries[h], (((1,), (1,)), ((), ())), preferred_element_type=jnp.float32
            ) * SCALE
            if masked:
                scores = jnp.where(allowed, scores, MASKED)
            new_peak = jnp.maximum(peak, jnp.max(scores, axis=0, keepdims=True))
            expon = jnp.exp2(scores - new_peak)
            if masked:
                expon = jnp.where(allowed, expon, 0.0)
            shrink = jnp.exp2(peak - new_peak)
            total = total * shrink + jnp.sum(expon, axis=0, keepdims=True)
            accum = accum * shrink + lax.dot_general(
                values,
                expon.astype(jnp.bfloat16),
                (((0,), (0,)), ((), ())),
                preferred_element_type=jnp.float32,
            )
            result.append((new_peak, total, accum))
        return tuple(result)

    state = tuple(
        (
            jnp.full((1, columns), MASKED, jnp.float32),
            jnp.zeros((1, columns), jnp.float32),
            jnp.zeros((HDIM, columns), jnp.float32),
        )
        for _ in range(heads)
    )
    inner = jnp.maximum((first + 1) // block_k, begin)
    clear = jnp.clip((high + block_k - 1) // block_k, begin, inner)
    state = lax.fori_loop(begin, clear, functools.partial(body, masked=True), state)
    state = lax.fori_loop(clear, inner, functools.partial(body, masked=False), state)
    state = lax.fori_loop(inner, end, functools.partial(body, masked=True), state)
    for h in range(heads):
        _, total, accum = state[h]
        rows = (accum / total).T.astype(jnp.bfloat16)
        out_ref[:, :, h * HDIM : (h + 1) * HDIM] = rows.reshape(slots, tile, HDIM)


def attend(queries, lower, key_values, first):
    slots, tokens, cols = queries.shape
    shards, kinds, rows, _ = key_values.shape
    heads = math.gcd(cols // HDIM, 2)
    tile = math.gcd(tokens, 256)
    block_k = math.gcd(rows, 512)
    by_tile = lower.reshape(tokens // tile, tile)
    bounds = jnp.concatenate(
        [first[None], jnp.stack([by_tile[:, 0], by_tile[:, -1]], axis=1).reshape(-1)]
    ).astype(jnp.int32)
    return pl.pallas_call(
        functools.partial(attention_kernel, block_k=block_k, heads=heads, tile=tile),
        grid=(cols // (heads * HDIM), tokens // tile),
        in_specs=[
            pl.BlockSpec(memory_space=pltpu.SMEM),
            pl.BlockSpec((slots, tile, heads * HDIM), lambda g, t: (0, t, g)),
            pl.BlockSpec((1, 1, tile), lambda g, t: (t, 0, 0)),
            pl.BlockSpec((shards, kinds, rows, heads * HDIM), lambda g, t: (0, 0, 0, g)),
        ],
        out_specs=pl.BlockSpec((slots, tile, heads * HDIM), lambda g, t: (0, t, g)),
        out_shape=jax.ShapeDtypeStruct((slots, tokens, cols), jnp.bfloat16),
        compiler_params=pltpu.CompilerParams(
            dimension_semantics=("arbitrary", "arbitrary"), vmem_limit_bytes=VMEM_BYTES
        ),
        cost_estimate=pl.CostEstimate(
            flops=4 * slots * tokens * cols * 2048,
            bytes_accessed=2 * (queries.size * 2 + key_values.size),
            transcendentals=slots * tokens * (cols // HDIM) * 2048,
        ),
        name="attend",
    )(bounds, queries, by_tile[:, None, :], key_values)


def out_kernel(x_ref, routes_ref, gates_ref, w_ref, out_ref, picked):
    experts = w_ref.shape[1]

    @pl.when(pl.program_id(0) == 0)
    def _():
        for e in range(experts):
            rows = jnp.zeros_like(x_ref[0])
            for slot in range(x_ref.shape[0]):
                rows = jnp.where(routes_ref[:, slot : slot + 1] == e, x_ref[slot], rows)
            picked[e] = rows

    total = jnp.zeros(out_ref.shape[1:], jnp.float32)
    for e in range(experts):
        term = jnp.dot(picked[e], w_ref[0, e], preferred_element_type=jnp.float32)
        total = total + gates_ref[:, e : e + 1] * term
    out_ref[0] = total.astype(jnp.bfloat16)


def project_out(attended, routes, gates, weight, parts):
    shards, experts, rows, cols = weight.shape
    slots, tokens, _ = attended.shape
    span = shards * cols // parts
    per = span // cols
    return pl.pallas_call(
        out_kernel,
        grid=(shards,),
        in_specs=[
            pl.BlockSpec((slots, tokens, rows), lambda i: (0, 0, 0)),
            pl.BlockSpec((tokens, slots), lambda i: (0, 0)),
            pl.BlockSpec((tokens, experts), lambda i: (0, 0)),
            pl.BlockSpec((1, experts, rows, cols), lambda i: (i, 0, 0, 0)),
        ],
        out_specs=pl.BlockSpec((1, tokens, cols), lambda i: (i // per, 0, i % per)),
        out_shape=jax.ShapeDtypeStruct((parts, tokens, span), jnp.bfloat16),
        scratch_shapes=[pltpu.VMEM((experts, tokens, rows), jnp.bfloat16)],
        compiler_params=params(),
        cost_estimate=pl.CostEstimate(
            flops=2 * experts * tokens * rows * shards * cols,
            bytes_accessed=2 * (weight.size + attended.size + tokens * shards * cols),
            transcendentals=0,
        ),
        name="project_out",
    )(attended, routes, gates, weight)


def local(
    hidden,
    segment_ids,
    routes,
    norm_gain,
    router_weight,
    query_weight,
    kv_weight,
    out_weight,
    page_table,
):
    tok_dev, width = hidden.shape
    head_cols = query_weight.shape[2]
    shards = lax.axis_size("tok")
    parts = lax.axis_size("mdl")
    tok_row = lax.axis_index("tok")
    pages_here = page_table.shape[0]
    page_rows = tok_dev // pages_here

    kv_full = lax.all_gather(kv_weight, "tok", axis=0)
    table = lax.all_gather(page_table, "tok", axis=0, tiled=True)
    normed = rms_norm(hidden, norm_gain)
    gates = route_gates(normed, router_weight, routes)
    key_values = lax.all_gather(project_kv(normed, kv_full), "tok", axis=0)
    query_full = lax.all_gather(query_weight, "tok", axis=0)
    out_full = lax.all_gather(out_weight, "tok", axis=0)

    here = tok_row * pages_here + jnp.arange(pages_here, dtype=jnp.int32)
    logical = jnp.arange(table.shape[0], dtype=jnp.int32)
    source = jnp.sum(jnp.where(table[None, :] == here[:, None], logical[None, :], 0), axis=1)
    paged = key_values.reshape(shards, 2, pages_here, page_rows, head_cols)
    cache = paged[source // pages_here, :, source % pages_here].transpose(0, 2, 1, 3)

    prompt_ids = jnp.arange(SEGS, dtype=jnp.int32)
    seg_first = jnp.sum((segment_ids[:, None] < prompt_ids[None, :]).astype(jnp.int32), axis=0)
    first = (tok_row * tok_dev).astype(jnp.int32)
    own_seg = lax.dynamic_slice_in_dim(segment_ids, first, tok_dev, 0)
    lower = jnp.sum(
        jnp.where(own_seg[:, None] == prompt_ids[None, :], seg_first[None, :], 0), axis=1
    )

    queries = project_queries(normed, routes, query_full)
    attended = attend(queries, lower, key_values, first)
    partial_sums = project_out(attended, routes, gates, out_full, parts)
    mine = lax.psum_scatter(partial_sums, "mdl", scatter_dimension=0, tiled=False)
    span = width // parts
    residual = lax.dynamic_slice_in_dim(hidden, lax.axis_index("mdl") * span, span, 1)
    output = (residual.astype(jnp.float32) + mine.astype(jnp.float32)).astype(jnp.bfloat16)
    return (output, cache)


def solution(mesh):
    placed = (
        P("tok", None),
        P(),
        P("tok", None),
        P(),
        P(),
        P(None, "tok", "mdl"),
        P(None, "tok", "mdl"),
        P(None, "mdl", "tok"),
        P("tok"),
    )
    return jax.shard_map(
        local,
        mesh=mesh,
        in_specs=placed,
        out_specs=(P("tok", "mdl"), P("tok", None, None, "mdl")),
        check_vma=False,
    )
```

```python
import functools
import math

import jax
import jax.numpy as jnp
from jax import lax
from jax.experimental import pallas as pl
from jax.experimental.pallas import tpu as pltpu
from jax.sharding import PartitionSpec as P

HDIM = 128
SEGS = 4
EPSILON = 1e-05
MASKED = -1e30
VMEM_BYTES = 48 * 1024 * 1024
SCALE = math.log2(math.e) / math.sqrt(HDIM)


def rms_norm(hidden, norm_gain):
    values = hidden.astype(jnp.float32)
    factor = lax.rsqrt(jnp.mean(values * values, axis=-1, keepdims=True) + EPSILON)
    return (values * factor * norm_gain).astype(jnp.bfloat16)


def route_gates(normed, router_weight, routes):
    logits = jnp.dot(normed.astype(jnp.float32), router_weight, precision=lax.Precision.HIGHEST)
    expert_ids = jnp.arange(logits.shape[1], dtype=jnp.int32)
    picked = routes[:, :, None] == expert_ids[None, None, :]
    chosen = jnp.sum(jnp.where(picked, logits[:, None, :], jnp.float32(0.0)), axis=-1)
    gates = jax.nn.softmax(chosen, axis=-1)
    return jnp.sum(jnp.where(picked, gates[:, :, None], jnp.float32(0.0)), axis=1)


def params():
    return pltpu.CompilerParams(
        dimension_semantics=("arbitrary",), vmem_limit_bytes=VMEM_BYTES
    )


def kv_kernel(x_ref, w_ref, out_ref):
    depth = w_ref.shape[0] * w_ref.shape[2]
    w = w_ref[:, 0].reshape(depth, w_ref.shape[3])
    out_ref[0] = jnp.dot(x_ref[...], w, preferred_element_type=jnp.float32).astype(jnp.bfloat16)


def project_kv(normed, weight):
    shards, kinds, rows, cols = weight.shape
    tokens, width = normed.shape
    return pl.pallas_call(
        kv_kernel,
        grid=(kinds,),
        in_specs=[
            pl.BlockSpec((tokens, width), lambda c: (0, 0)),
            pl.BlockSpec((shards, 1, rows, cols), lambda c: (0, c, 0, 0)),
        ],
        out_specs=pl.BlockSpec((1, tokens, cols), lambda c: (c, 0, 0)),
        out_shape=jax.ShapeDtypeStruct((kinds, tokens, cols), jnp.bfloat16),
        compiler_params=params(),
        cost_estimate=pl.CostEstimate(
            flops=2 * kinds * tokens * width * cols,
            bytes_accessed=2 * (weight.size + normed.size + kinds * tokens * cols),
            transcendentals=0,
        ),
        name="project_kv",
    )(normed, weight)


def query_kernel(x_ref, routes_ref, w_ref, out_ref):
    expert = pl.program_id(0)
    depth = w_ref.shape[0] * w_ref.shape[2]
    w = w_ref[:, 0].reshape(depth, w_ref.shape[3])
    y = jnp.dot(x_ref[...], w, preferred_element_type=jnp.float32).astype(jnp.bfloat16)

    @pl.when(expert == 0)
    def _():
        out_ref[...] = jnp.zeros_like(out_ref)

    for slot in range(out_ref.shape[0]):
        mine = routes_ref[:, slot : slot + 1] == expert
        out_ref[slot] = jnp.where(mine, y, out_ref[slot])


def project_queries(normed, routes, weight):
    shards, experts, rows, cols = weight.shape
    tokens, width = normed.shape
    slots = routes.shape[1]
    return pl.pallas_call(
        query_kernel,
        grid=(experts,),
        in_specs=[
            pl.BlockSpec((tokens, width), lambda e: (0, 0)),
            pl.BlockSpec((tokens, slots), lambda e: (0, 0)),
            pl.BlockSpec((shards, 1, rows, cols), lambda e: (0, e, 0, 0)),
        ],
        out_specs=pl.BlockSpec((slots, tokens, cols), lambda e: (0, 0, 0)),
        out_shape=jax.ShapeDtypeStruct((slots, tokens, cols), jnp.bfloat16),
        compiler_params=params(),
        cost_estimate=pl.CostEstimate(
            flops=2 * experts * tokens * width * cols,
            bytes_accessed=2 * (weight.size + normed.size + slots * tokens * cols),
            transcendentals=0,
        ),
        name="project_queries",
    )(normed, routes, weight)


def attention_kernel(bounds_ref, q_ref, lower_ref, kv_ref, out_ref, *, block_k, heads, tile):
    pos_first = bounds_ref[0]
    step = pl.program_id(1)
    first = pos_first + step * tile
    low = bounds_ref[1 + 2 * step]
    high = bounds_ref[2 + 2 * step]
    slots = q_ref.shape[0]
    columns = slots * tile
    per_shard = kv_ref.shape[2] // block_k
    begin = low // block_k
    end = (first + tile - 1) // block_k + 1
    q_pos = first + lax.broadcasted_iota(jnp.int32, (1, columns), 1) % tile
    lower = jnp.concatenate([lower_ref[0]] * slots, axis=1)
    queries = [
        q_ref[:, :, h * HDIM : (h + 1) * HDIM].reshape(columns, HDIM) for h in range(heads)
    ]

    def body(block, carry, masked):
        shard = block // per_shard
        rows = pl.ds((block % per_shard) * block_k, block_k)
        if masked:
            k_pos = block * block_k + lax.broadcasted_iota(jnp.int32, (block_k, columns), 0)
            allowed = (k_pos >= lower) & (k_pos <= q_pos)
        result = []
        for h in range(heads):
            peak, total, accum = carry[h]
            span = slice(h * HDIM, (h + 1) * HDIM)
            keys = kv_ref[shard, 0, rows, span]
            values = kv_ref[shard, 1, rows, span]
            scores = lax.dot_general(
                keys, queries[h], (((1,), (1,)), ((), ())), preferred_element_type=jnp.float32
            ) * SCALE
            if masked:
                scores = jnp.where(allowed, scores, MASKED)
            new_peak = jnp.maximum(peak, jnp.max(scores, axis=0, keepdims=True))
            expon = jnp.exp2(scores - new_peak)
            if masked:
                expon = jnp.where(allowed, expon, 0.0)
            shrink = jnp.exp2(peak - new_peak)
            total = total * shrink + jnp.sum(expon, axis=0, keepdims=True)
            accum = accum * shrink + lax.dot_general(
                values,
                expon.astype(jnp.bfloat16),
                (((0,), (0,)), ((), ())),
                preferred_element_type=jnp.float32,
            )
            result.append((new_peak, total, accum))
        return tuple(result)

    state = tuple(
        (
            jnp.full((1, columns), MASKED, jnp.float32),
            jnp.zeros((1, columns), jnp.float32),
            jnp.zeros((HDIM, columns), jnp.float32),
        )
        for _ in range(heads)
    )
    inner = jnp.maximum((first + 1) // block_k, begin)
    clear = jnp.clip((high + block_k - 1) // block_k, begin, inner)
    state = lax.fori_loop(begin, clear, functools.partial(body, masked=True), state)
    state = lax.fori_loop(clear, inner, functools.partial(body, masked=False), state)
    state = lax.fori_loop(inner, end, functools.partial(body, masked=True), state)
    for h in range(heads):
        _, total, accum = state[h]
        rows = (accum / total).T.astype(jnp.bfloat16)
        out_ref[:, :, h * HDIM : (h + 1) * HDIM] = rows.reshape(slots, tile, HDIM)


def attend(queries, lower, key_values, first):
    slots, tokens, cols = queries.shape
    shards, kinds, rows, _ = key_values.shape
    heads = math.gcd(cols // HDIM, 2)
    tile = math.gcd(tokens, 256)
    block_k = math.gcd(rows, 512)
    by_tile = lower.reshape(tokens // tile, tile)
    bounds = jnp.concatenate(
        [first[None], jnp.stack([by_tile[:, 0], by_tile[:, -1]], axis=1).reshape(-1)]
    ).astype(jnp.int32)
    return pl.pallas_call(
        functools.partial(attention_kernel, block_k=block_k, heads=heads, tile=tile),
        grid=(cols // (heads * HDIM), tokens // tile),
        in_specs=[
            pl.BlockSpec(memory_space=pltpu.SMEM),
            pl.BlockSpec((slots, tile, heads * HDIM), lambda g, t: (0, t, g)),
            pl.BlockSpec((1, 1, tile), lambda g, t: (t, 0, 0)),
            pl.BlockSpec((shards, kinds, rows, heads * HDIM), lambda g, t: (0, 0, 0, g)),
        ],
        out_specs=pl.BlockSpec((slots, tile, heads * HDIM), lambda g, t: (0, t, g)),
        out_shape=jax.ShapeDtypeStruct((slots, tokens, cols), jnp.bfloat16),
        compiler_params=pltpu.CompilerParams(
            dimension_semantics=("arbitrary", "arbitrary"), vmem_limit_bytes=VMEM_BYTES
        ),
        cost_estimate=pl.CostEstimate(
            flops=4 * slots * tokens * cols * 2048,
            bytes_accessed=2 * (queries.size * 2 + key_values.size),
            transcendentals=slots * tokens * (cols // HDIM) * 2048,
        ),
        name="attend",
    )(bounds, queries, by_tile[:, None, :], key_values)


def out_kernel(x_ref, routes_ref, gates_ref, w_ref, out_ref, picked):
    experts = w_ref.shape[1]

    @pl.when(pl.program_id(0) == 0)
    def _():
        for e in range(experts):
            rows = jnp.zeros_like(x_ref[0])
            for slot in range(x_ref.shape[0]):
                rows = jnp.where(routes_ref[:, slot : slot + 1] == e, x_ref[slot], rows)
            picked[e] = rows

    total = jnp.zeros(out_ref.shape[1:], jnp.float32)
    for e in range(experts):
        term = jnp.dot(picked[e], w_ref[0, e], preferred_element_type=jnp.float32)
        total = total + gates_ref[:, e : e + 1] * term
    out_ref[0] = total.astype(jnp.bfloat16)


def project_out(attended, routes, gates, weight, parts):
    shards, experts, rows, cols = weight.shape
    slots, tokens, _ = attended.shape
    span = shards * cols // parts
    per = span // cols
    return pl.pallas_call(
        out_kernel,
        grid=(shards,),
        in_specs=[
            pl.BlockSpec((slots, tokens, rows), lambda i: (0, 0, 0)),
            pl.BlockSpec((tokens, slots), lambda i: (0, 0)),
            pl.BlockSpec((tokens, experts), lambda i: (0, 0)),
            pl.BlockSpec((1, experts, rows, cols), lambda i: (i, 0, 0, 0)),
        ],
        out_specs=pl.BlockSpec((1, tokens, cols), lambda i: (i // per, 0, i % per)),
        out_shape=jax.ShapeDtypeStruct((parts, tokens, span), jnp.bfloat16),
        scratch_shapes=[pltpu.VMEM((experts, tokens, rows), jnp.bfloat16)],
        compiler_params=params(),
        cost_estimate=pl.CostEstimate(
            flops=2 * experts * tokens * rows * shards * cols,
            bytes_accessed=2 * (weight.size + attended.size + tokens * shards * cols),
            transcendentals=0,
        ),
        name="project_out",
    )(attended, routes, gates, weight)


def gather_kernel(
    x_ref,
    routes_ref,
    kvw_ref,
    qw_ref,
    q_ref,
    gathered_ref,
    weights,
    own_kv,
    send_sem,
    recv_sem,
    local_sem,
):
    me = lax.axis_index("tok")
    core, col, row = me % 2, (me // 2) % 2, me // 4
    to_core, to_col, to_row = 1 - 2 * core, 2 - 4 * col, 4 - 8 * row
    mate, side, over = me + to_core, me + to_col, me + to_row
    across = me + to_col + to_row

    barrier = pltpu.get_barrier_semaphore()
    for other in (mate, side, over):
        pl.semaphore_signal(
            barrier, inc=1, device_id={"tok": other}, device_id_type=pl.DeviceIdType.MESH
        )
    pl.semaphore_wait(barrier, 3)

    kinds, experts = kvw_ref.shape[0], qw_ref.shape[0]
    early = min(2, experts)
    order = [("w", c) for c in range(kinds + early)]
    order += [("kv", c) for c in range(kinds)]
    order += [("w", c) for c in range(kinds + early, kinds + experts)]
    count = len(order)

    def source(chunk):
        kind, c = chunk
        if kind == "kv":
            return own_kv.at[c]
        return kvw_ref.at[c] if c < kinds else qw_ref.at[c - kinds]

    def slot(chunk, shard):
        kind, c = chunk
        return gathered_ref.at[shard, c] if kind == "kv" else weights.at[c, shard]

    def half(ref, part):
        rows = ref.shape[0] // 2
        return ref.at[pl.ds(part * rows, rows)]

    def copy(k, way, src, dst, other):
        return pltpu.make_async_remote_copy(
            src_ref=src,
            dst_ref=dst,
            send_sem=send_sem.at[k, way],
            recv_sem=recv_sem.at[k, way],
            device_id={"tok": other},
            device_id_type=pl.DeviceIdType.MESH,
        )

    def send(k, way):
        chunk = order[k]
        if way < 3:
            return copy(k, way, source(chunk), slot(chunk, me), (mate, side, over)[way])
        place, other = [
            (half(slot(chunk, over), 0), side),
            (half(slot(chunk, side), 1), over),
            (slot(chunk, side), mate),
            (slot(chunk, over), mate),
            (slot(chunk, across), mate),
        ][way - 3]
        return copy(k, way, place, place, other)

    def arrival(k, way):
        chunk = order[k]
        place = [
            slot(chunk, mate),
            slot(chunk, side),
            slot(chunk, over),
            half(slot(chunk, across), 0),
            half(slot(chunk, across), 1),
            slot(chunk, side + to_core),
            slot(chunk, over + to_core),
            slot(chunk, across + to_core),
        ][way]
        return copy(k, way, place, place, mate)

    def keep(k):
        return pltpu.make_async_copy(source(order[k]), slot(order[k], me), local_sem.at[k])

    def project(c):
        depth = weights.shape[1] * weights.shape[2]
        w = weights[c].reshape(depth, weights.shape[3])
        return jnp.dot(x_ref[...], w, preferred_element_type=jnp.float32).astype(jnp.bfloat16)

    def finish(k):
        kind, c = order[k]
        for way in (0, 5, 6, 7):
            arrival(k, way).wait_recv()
        keep(k).wait()
        if kind == "kv":
            return
        y = project(c)
        if c < kinds:
            own_kv[c] = y
            return
        expert = c - kinds
        for s in range(q_ref.shape[0]):
            mine = routes_ref[:, s : s + 1] == expert
            before = jnp.zeros_like(y) if expert == 0 else q_ref[s]
            q_ref[s] = jnp.where(mine, y, before)

    for k in range(count + 3):
        if k < count:
            for way in (1, 2, 0):
                send(k, way).start()
            keep(k).start()
        j = k - 1
        if 0 <= j < count:
            arrival(j, 1).wait_recv()
            send(j, 4).start()
            send(j, 5).start()
            arrival(j, 2).wait_recv()
            send(j, 3).start()
            send(j, 6).start()
        j = k - 2
        if 0 <= j < count:
            arrival(j, 3).wait_recv()
            arrival(j, 4).wait_recv()
            send(j, 7).start()
        j = k - 3
        if 0 <= j < count:
            finish(j)
    for k in range(count):
        for way in range(8):
            send(k, way).wait_send()


def gather_project(normed, routes, kv_weight, query_weight, shards):
    tokens, width = normed.shape
    kinds, rows, cols = kv_weight.shape
    experts = query_weight.shape[0]
    slots = routes.shape[1]
    chunks = 2 * kinds + experts
    vmem = pl.BlockSpec(memory_space=pltpu.VMEM)
    anywhere = pl.BlockSpec(memory_space=pl.ANY)
    return pl.pallas_call(
        gather_kernel,
        in_specs=[vmem, vmem, anywhere, anywhere],
        out_specs=[vmem, anywhere],
        out_shape=[
            jax.ShapeDtypeStruct((slots, tokens, cols), jnp.bfloat16),
            jax.ShapeDtypeStruct((shards, kinds, tokens, cols), jnp.bfloat16),
        ],
        scratch_shapes=[
            pltpu.VMEM((kinds + experts, shards, rows, cols), jnp.bfloat16),
            pltpu.VMEM((kinds, tokens, cols), jnp.bfloat16),
            pltpu.SemaphoreType.DMA((chunks, 8)),
            pltpu.SemaphoreType.DMA((chunks, 8)),
            pltpu.SemaphoreType.DMA((chunks,)),
        ],
        compiler_params=pltpu.CompilerParams(
            collective_id=1, has_side_effects=True, vmem_limit_bytes=VMEM_BYTES
        ),
        cost_estimate=pl.CostEstimate(
            flops=2 * (kinds + experts) * tokens * width * cols * 10,
            bytes_accessed=200 * 1024 * 1024,
            transcendentals=0,
        ),
        name="gather_project",
    )(normed, routes, kv_weight, query_weight)


def out_sum_kernel(
    x_ref,
    routes_ref,
    gates_ref,
    hidden_ref,
    w_ref,
    out_ref,
    weights,
    picked,
    own,
    near,
    far,
    load_sem,
    send_sem,
    recv_sem,
):
    me = lax.axis_index("mdl")
    low, high = me % 2, me // 2
    near_id, far_id = me + 1 - 2 * low, me + 2 - 4 * high
    both = near_id + 2 - 4 * high
    shards, experts = w_ref.shape[:2]
    cols = w_ref.shape[3]
    per = shards // 4
    targets = [both, near_id, far_id, me]

    def load(n):
        index = targets[n // per] * per + n % per
        return pltpu.make_async_copy(w_ref.at[index], weights.at[n], load_sem.at[n])

    for n in range(shards):
        load(n).start()

    barrier = pltpu.get_barrier_semaphore()
    for other in (near_id, far_id):
        pl.semaphore_signal(
            barrier, inc=1, device_id={"mdl": other}, device_id_type=pl.DeviceIdType.MESH
        )
    pl.semaphore_wait(barrier, 2)

    for e in range(experts):
        rows = jnp.zeros_like(x_ref[0])
        for s in range(x_ref.shape[0]):
            rows = jnp.where(routes_ref[:, s : s + 1] == e, x_ref[s], rows)
        picked[e] = rows

    def copy(way, src, dst, other):
        return pltpu.make_async_remote_copy(
            src_ref=src,
            dst_ref=dst,
            send_sem=send_sem.at[way],
            recv_sem=recv_sem.at[way],
            device_id={"mdl": other},
            device_id_type=pl.DeviceIdType.MESH,
        )

    def near_copy(way):
        return copy(way, own.at[way], near.at[way], near_id)

    def far_copy():
        return copy(2, own.at[2], far, far_id)

    def block(n, piece):
        load(n * per + piece).wait()
        total = jnp.zeros((own.shape[1], cols), jnp.float32)
        for e in range(experts):
            term = jnp.dot(picked[e], weights[n * per + piece, e], preferred_element_type=jnp.float32)
            total = total + gates_ref[:, e : e + 1] * term
        return total

    for n in range(4):
        for piece in range(per):
            span = slice(piece * cols, (piece + 1) * cols)
            own[n, :, span] = block(n, piece).astype(jnp.bfloat16)
        if n < 2:
            near_copy(n).start()
        elif n == 2:
            near_copy(0).wait_recv()
            own[2] = (own[2].astype(jnp.float32) + near[0].astype(jnp.float32)).astype(jnp.bfloat16)
            far_copy().start()
    near_copy(1).wait_recv()
    part = own[3].astype(jnp.float32) + near[1].astype(jnp.float32) + hidden_ref[...].astype(jnp.float32)
    far_copy().wait_recv()
    out_ref[...] = (part + far[...].astype(jnp.float32)).astype(jnp.bfloat16)
    near_copy(0).wait_send()
    near_copy(1).wait_send()
    far_copy().wait_send()


def project_out_sum(attended, routes, gates, residual, weight):
    shards, experts, rows, cols = weight.shape
    _, tokens, _ = attended.shape
    span = shards * cols // 4
    vmem = pl.BlockSpec(memory_space=pltpu.VMEM)
    return pl.pallas_call(
        out_sum_kernel,
        in_specs=[vmem, vmem, vmem, vmem, pl.BlockSpec(memory_space=pl.ANY)],
        out_specs=vmem,
        out_shape=jax.ShapeDtypeStruct((tokens, span), jnp.bfloat16),
        scratch_shapes=[
            pltpu.VMEM((shards, experts, rows, cols), jnp.bfloat16),
            pltpu.VMEM((experts, tokens, rows), jnp.bfloat16),
            pltpu.VMEM((4, tokens, span), jnp.bfloat16),
            pltpu.VMEM((2, tokens, span), jnp.bfloat16),
            pltpu.VMEM((tokens, span), jnp.bfloat16),
            pltpu.SemaphoreType.DMA((shards,)),
            pltpu.SemaphoreType.DMA((3,)),
            pltpu.SemaphoreType.DMA((3,)),
        ],
        compiler_params=pltpu.CompilerParams(
            collective_id=2, has_side_effects=True, vmem_limit_bytes=VMEM_BYTES
        ),
        cost_estimate=pl.CostEstimate(
            flops=2 * experts * tokens * rows * shards * cols,
            bytes_accessed=2 * weight.size,
            transcendentals=0,
        ),
        name="project_out_sum",
    )(attended, routes, gates, residual, weight)


def local(
    hidden,
    segment_ids,
    routes,
    norm_gain,
    router_weight,
    query_weight,
    kv_weight,
    out_weight,
    page_table,
):
    tok_dev, width = hidden.shape
    head_cols = query_weight.shape[2]
    shards = lax.axis_size("tok")
    parts = lax.axis_size("mdl")
    tok_row = lax.axis_index("tok")
    pages_here = page_table.shape[0]
    page_rows = tok_dev // pages_here

    own_kernels = shards == 8 and parts == 4
    table = lax.all_gather(page_table, "tok", axis=0, tiled=True)
    normed = rms_norm(hidden, norm_gain)
    gates = route_gates(normed, router_weight, routes)
    out_full = lax.all_gather(out_weight, "tok", axis=0)
    if own_kernels:
        queries, key_values = gather_project(normed, routes, kv_weight, query_weight, shards)
    else:
        kv_full = lax.all_gather(kv_weight, "tok", axis=0)
        key_values = lax.all_gather(project_kv(normed, kv_full), "tok", axis=0)
        query_full = lax.all_gather(query_weight, "tok", axis=0)
        queries = project_queries(normed, routes, query_full)

    here = tok_row * pages_here + jnp.arange(pages_here, dtype=jnp.int32)
    logical = jnp.arange(table.shape[0], dtype=jnp.int32)
    source = jnp.sum(jnp.where(table[None, :] == here[:, None], logical[None, :], 0), axis=1)
    paged = key_values.reshape(shards, 2, pages_here, page_rows, head_cols)
    cache = paged[source // pages_here, :, source % pages_here].transpose(0, 2, 1, 3)

    prompt_ids = jnp.arange(SEGS, dtype=jnp.int32)
    seg_first = jnp.sum((segment_ids[:, None] < prompt_ids[None, :]).astype(jnp.int32), axis=0)
    first = (tok_row * tok_dev).astype(jnp.int32)
    own_seg = lax.dynamic_slice_in_dim(segment_ids, first, tok_dev, 0)
    lower = jnp.sum(
        jnp.where(own_seg[:, None] == prompt_ids[None, :], seg_first[None, :], 0), axis=1
    )

    attended = attend(queries, lower, key_values, first)
    span = width // parts
    residual = lax.dynamic_slice_in_dim(hidden, lax.axis_index("mdl") * span, span, 1)
    if own_kernels:
        return (project_out_sum(attended, routes, gates, residual, out_full), cache)
    partial_sums = project_out(attended, routes, gates, out_full, parts)
    mine = lax.psum_scatter(partial_sums, "mdl", scatter_dimension=0, tiled=False)
    output = (residual.astype(jnp.float32) + mine.astype(jnp.float32)).astype(jnp.bfloat16)
    return (output, cache)


def solution(mesh):
    placed = (
        P("tok", None),
        P(),
        P("tok", None),
        P(),
        P(),
        P(None, "tok", "mdl"),
        P(None, "tok", "mdl"),
        P(None, "mdl", "tok"),
        P("tok"),
    )
    return jax.shard_map(
        local,
        mesh=mesh,
        in_specs=placed,
        out_specs=(P("tok", "mdl"), P("tok", None, None, "mdl")),
        check_vma=False,
    )
```

```python
import functools
import math

import jax
import jax.numpy as jnp
from jax import lax
from jax.experimental import pallas as pl
from jax.experimental.pallas import tpu as pltpu
from jax.sharding import PartitionSpec as P

HDIM = 128
SEGS = 4
EPSILON = 1e-05
MASKED = -1e30
VMEM_BYTES = 48 * 1024 * 1024
LARGE_VMEM_BYTES = 60 * 1024 * 1024
SCALE = math.log2(math.e) / math.sqrt(HDIM)


def rms_norm(hidden, norm_gain):
    values = hidden.astype(jnp.float32)
    factor = lax.rsqrt(jnp.mean(values * values, axis=-1, keepdims=True) + EPSILON)
    return (values * factor * norm_gain).astype(jnp.bfloat16)


def route_gates(normed, router_weight, routes):
    logits = jnp.dot(normed.astype(jnp.float32), router_weight, precision=lax.Precision.HIGHEST)
    expert_ids = jnp.arange(logits.shape[1], dtype=jnp.int32)
    picked = routes[:, :, None] == expert_ids[None, None, :]
    chosen = jnp.sum(jnp.where(picked, logits[:, None, :], jnp.float32(0.0)), axis=-1)
    gates = jax.nn.softmax(chosen, axis=-1)
    return jnp.sum(jnp.where(picked, gates[:, :, None], jnp.float32(0.0)), axis=1)


def params():
    return pltpu.CompilerParams(
        dimension_semantics=("arbitrary",), vmem_limit_bytes=VMEM_BYTES
    )


def kv_kernel(x_ref, w_ref, out_ref):
    depth = w_ref.shape[0] * w_ref.shape[2]
    w = w_ref[:, 0].reshape(depth, w_ref.shape[3])
    out_ref[0] = jnp.dot(x_ref[...], w, preferred_element_type=jnp.float32).astype(jnp.bfloat16)


def project_kv(normed, weight):
    shards, kinds, rows, cols = weight.shape
    tokens, width = normed.shape
    return pl.pallas_call(
        kv_kernel,
        grid=(kinds,),
        in_specs=[
            pl.BlockSpec((tokens, width), lambda c: (0, 0)),
            pl.BlockSpec((shards, 1, rows, cols), lambda c: (0, c, 0, 0)),
        ],
        out_specs=pl.BlockSpec((1, tokens, cols), lambda c: (c, 0, 0)),
        out_shape=jax.ShapeDtypeStruct((kinds, tokens, cols), jnp.bfloat16),
        compiler_params=params(),
        cost_estimate=pl.CostEstimate(
            flops=2 * kinds * tokens * width * cols,
            bytes_accessed=2 * (weight.size + normed.size + kinds * tokens * cols),
            transcendentals=0,
        ),
        name="project_kv",
    )(normed, weight)


def query_kernel(x_ref, routes_ref, w_ref, out_ref):
    expert = pl.program_id(0)
    depth = w_ref.shape[0] * w_ref.shape[2]
    w = w_ref[:, 0].reshape(depth, w_ref.shape[3])
    y = jnp.dot(x_ref[...], w, preferred_element_type=jnp.float32).astype(jnp.bfloat16)

    @pl.when(expert == 0)
    def _():
        out_ref[...] = jnp.zeros_like(out_ref)

    for slot in range(out_ref.shape[0]):
        mine = routes_ref[:, slot : slot + 1] == expert
        out_ref[slot] = jnp.where(mine, y, out_ref[slot])


def project_queries(normed, routes, weight):
    shards, experts, rows, cols = weight.shape
    tokens, width = normed.shape
    slots = routes.shape[1]
    return pl.pallas_call(
        query_kernel,
        grid=(experts,),
        in_specs=[
            pl.BlockSpec((tokens, width), lambda e: (0, 0)),
            pl.BlockSpec((tokens, slots), lambda e: (0, 0)),
            pl.BlockSpec((shards, 1, rows, cols), lambda e: (0, e, 0, 0)),
        ],
        out_specs=pl.BlockSpec((slots, tokens, cols), lambda e: (0, 0, 0)),
        out_shape=jax.ShapeDtypeStruct((slots, tokens, cols), jnp.bfloat16),
        compiler_params=params(),
        cost_estimate=pl.CostEstimate(
            flops=2 * experts * tokens * width * cols,
            bytes_accessed=2 * (weight.size + normed.size + slots * tokens * cols),
            transcendentals=0,
        ),
        name="project_queries",
    )(normed, routes, weight)


def attention_kernel(bounds_ref, q_ref, lower_ref, kv_ref, out_ref, *, block_k, heads, tile):
    pos_first = bounds_ref[0]
    step = pl.program_id(1)
    first = pos_first + step * tile
    low = bounds_ref[1 + 2 * step]
    high = bounds_ref[2 + 2 * step]
    slots = q_ref.shape[0]
    columns = slots * tile
    per_shard = kv_ref.shape[2] // block_k
    begin = low // block_k
    end = (first + tile - 1) // block_k + 1
    q_pos = first + lax.broadcasted_iota(jnp.int32, (1, columns), 1) % tile
    lower = jnp.concatenate([lower_ref[0]] * slots, axis=1)
    queries = [
        q_ref[:, :, h * HDIM : (h + 1) * HDIM].reshape(columns, HDIM) for h in range(heads)
    ]

    def body(block, carry, masked):
        shard = block // per_shard
        rows = pl.ds((block % per_shard) * block_k, block_k)
        if masked:
            k_pos = block * block_k + lax.broadcasted_iota(jnp.int32, (block_k, columns), 0)
            allowed = (k_pos >= lower) & (k_pos <= q_pos)
        result = []
        for h in range(heads):
            peak, total, accum = carry[h]
            span = slice(h * HDIM, (h + 1) * HDIM)
            keys = kv_ref[shard, 0, rows, span]
            values = kv_ref[shard, 1, rows, span]
            scores = lax.dot_general(
                keys, queries[h], (((1,), (1,)), ((), ())), preferred_element_type=jnp.float32
            ) * SCALE
            if masked:
                scores = jnp.where(allowed, scores, MASKED)
            new_peak = jnp.maximum(peak, jnp.max(scores, axis=0, keepdims=True))
            expon = jnp.exp2(scores - new_peak)
            if masked:
                expon = jnp.where(allowed, expon, 0.0)
            shrink = jnp.exp2(peak - new_peak)
            total = total * shrink + jnp.sum(expon, axis=0, keepdims=True)
            accum = accum * shrink + lax.dot_general(
                values,
                expon.astype(jnp.bfloat16),
                (((0,), (0,)), ((), ())),
                preferred_element_type=jnp.float32,
            )
            result.append((new_peak, total, accum))
        return tuple(result)

    state = tuple(
        (
            jnp.full((1, columns), MASKED, jnp.float32),
            jnp.zeros((1, columns), jnp.float32),
            jnp.zeros((HDIM, columns), jnp.float32),
        )
        for _ in range(heads)
    )
    inner = jnp.maximum((first + 1) // block_k, begin)
    clear = jnp.clip((high + block_k - 1) // block_k, begin, inner)
    state = lax.fori_loop(begin, clear, functools.partial(body, masked=True), state)
    state = lax.fori_loop(clear, inner, functools.partial(body, masked=False), state)
    state = lax.fori_loop(inner, end, functools.partial(body, masked=True), state)
    for h in range(heads):
        _, total, accum = state[h]
        rows = (accum / total).T.astype(jnp.bfloat16)
        out_ref[:, :, h * HDIM : (h + 1) * HDIM] = rows.reshape(slots, tile, HDIM)


def attend(queries, lower, key_values, first):
    slots, tokens, cols = queries.shape
    shards, kinds, rows, _ = key_values.shape
    heads = math.gcd(cols // HDIM, 2)
    tile = math.gcd(tokens, 256)
    block_k = math.gcd(rows, 512)
    by_tile = lower.reshape(tokens // tile, tile)
    bounds = jnp.concatenate(
        [first[None], jnp.stack([by_tile[:, 0], by_tile[:, -1]], axis=1).reshape(-1)]
    ).astype(jnp.int32)
    return pl.pallas_call(
        functools.partial(attention_kernel, block_k=block_k, heads=heads, tile=tile),
        grid=(cols // (heads * HDIM), tokens // tile),
        in_specs=[
            pl.BlockSpec(memory_space=pltpu.SMEM),
            pl.BlockSpec((slots, tile, heads * HDIM), lambda g, t: (0, t, g)),
            pl.BlockSpec((1, 1, tile), lambda g, t: (t, 0, 0)),
            pl.BlockSpec((shards, kinds, rows, heads * HDIM), lambda g, t: (0, 0, 0, g)),
        ],
        out_specs=pl.BlockSpec((slots, tile, heads * HDIM), lambda g, t: (0, t, g)),
        out_shape=jax.ShapeDtypeStruct((slots, tokens, cols), jnp.bfloat16),
        compiler_params=pltpu.CompilerParams(
            dimension_semantics=("arbitrary", "arbitrary"), vmem_limit_bytes=VMEM_BYTES
        ),
        cost_estimate=pl.CostEstimate(
            flops=4 * slots * tokens * cols * 2048,
            bytes_accessed=2 * (queries.size * 2 + key_values.size),
            transcendentals=slots * tokens * (cols // HDIM) * 2048,
        ),
        name="attend",
    )(bounds, queries, by_tile[:, None, :], key_values)


def out_kernel(x_ref, routes_ref, gates_ref, w_ref, out_ref, picked):
    experts = w_ref.shape[1]

    @pl.when(pl.program_id(0) == 0)
    def _():
        for e in range(experts):
            rows = jnp.zeros_like(x_ref[0])
            for slot in range(x_ref.shape[0]):
                rows = jnp.where(routes_ref[:, slot : slot + 1] == e, x_ref[slot], rows)
            picked[e] = rows

    total = jnp.zeros(out_ref.shape[1:], jnp.float32)
    for e in range(experts):
        term = jnp.dot(picked[e], w_ref[0, e], preferred_element_type=jnp.float32)
        total = total + gates_ref[:, e : e + 1] * term
    out_ref[0] = total.astype(jnp.bfloat16)


def project_out(attended, routes, gates, weight, parts):
    shards, experts, rows, cols = weight.shape
    slots, tokens, _ = attended.shape
    span = shards * cols // parts
    per = span // cols
    return pl.pallas_call(
        out_kernel,
        grid=(shards,),
        in_specs=[
            pl.BlockSpec((slots, tokens, rows), lambda i: (0, 0, 0)),
            pl.BlockSpec((tokens, slots), lambda i: (0, 0)),
            pl.BlockSpec((tokens, experts), lambda i: (0, 0)),
            pl.BlockSpec((1, experts, rows, cols), lambda i: (i, 0, 0, 0)),
        ],
        out_specs=pl.BlockSpec((1, tokens, cols), lambda i: (i // per, 0, i % per)),
        out_shape=jax.ShapeDtypeStruct((parts, tokens, span), jnp.bfloat16),
        scratch_shapes=[pltpu.VMEM((experts, tokens, rows), jnp.bfloat16)],
        compiler_params=params(),
        cost_estimate=pl.CostEstimate(
            flops=2 * experts * tokens * rows * shards * cols,
            bytes_accessed=2 * (weight.size + attended.size + tokens * shards * cols),
            transcendentals=0,
        ),
        name="project_out",
    )(attended, routes, gates, weight)


class TokRing:
    def __init__(self, order, send_sem, recv_sem, local_sem):
        me = lax.axis_index("tok")
        core, col, row = me % 2, (me // 2) % 2, me // 4
        to_core, to_col, to_row = 1 - 2 * core, 2 - 4 * col, 4 - 8 * row
        self.me, self.to_core = me, to_core
        self.mate, self.side, self.over = me + to_core, me + to_col, me + to_row
        self.across = me + to_col + to_row
        self.order = order
        self.send_sem, self.recv_sem, self.local_sem = send_sem, recv_sem, local_sem

    def greet(self):
        barrier = pltpu.get_barrier_semaphore()
        for other in (self.mate, self.side, self.over):
            pl.semaphore_signal(
                barrier, inc=1, device_id={"tok": other}, device_id_type=pl.DeviceIdType.MESH
            )
        pl.semaphore_wait(barrier, 3)

    def half(self, ref, part):
        rows = ref.shape[0] // 2
        return ref.at[pl.ds(part * rows, rows)]

    def copy(self, k, way, src, dst, other):
        return pltpu.make_async_remote_copy(
            src_ref=src,
            dst_ref=dst,
            send_sem=self.send_sem.at[k, way],
            recv_sem=self.recv_sem.at[k, way],
            device_id={"tok": other},
            device_id_type=pl.DeviceIdType.MESH,
        )

    def send(self, k, way):
        own, slot = self.order[k]
        if way < 3:
            return self.copy(k, way, own, slot(self.me), (self.mate, self.side, self.over)[way])
        place, other = [
            lambda: (self.half(slot(self.over), 0), self.side),
            lambda: (self.half(slot(self.side), 1), self.over),
            lambda: (slot(self.side), self.mate),
            lambda: (slot(self.over), self.mate),
            lambda: (slot(self.across), self.mate),
        ][way - 3]()
        return self.copy(k, way, place, place, other)

    def arrival(self, k, way):
        slot = self.order[k][1]
        place = [
            lambda: slot(self.mate),
            lambda: slot(self.side),
            lambda: slot(self.over),
            lambda: self.half(slot(self.across), 0),
            lambda: self.half(slot(self.across), 1),
            lambda: slot(self.side + self.to_core),
            lambda: slot(self.over + self.to_core),
            lambda: slot(self.across + self.to_core),
        ][way]()
        return self.copy(k, way, place, place, self.mate)

    def keep(self, k):
        own, slot = self.order[k]
        return pltpu.make_async_copy(own, slot(self.me), self.local_sem.at[k])

    def begin(self, k):
        for way in (1, 2, 0):
            self.send(k, way).start()
        self.keep(k).start()

    def forward(self, k):
        self.arrival(k, 1).wait_recv()
        self.send(k, 4).start()
        self.send(k, 5).start()
        self.arrival(k, 2).wait_recv()
        self.send(k, 3).start()
        self.send(k, 6).start()

    def share(self, k):
        self.arrival(k, 3).wait_recv()
        self.arrival(k, 4).wait_recv()
        self.send(k, 7).start()

    def complete(self, k):
        for way in (0, 5, 6, 7):
            self.arrival(k, way).wait_recv()
        self.keep(k).wait()

    def step(self, k, finish=None):
        count = len(self.order)
        if k < count:
            self.begin(k)
        if 0 <= k - 1 < count:
            self.forward(k - 1)
        if 0 <= k - 2 < count:
            self.share(k - 2)
        if 0 <= k - 3 < count:
            self.complete(k - 3)
            if finish is not None:
                finish(k - 3)

    def drain(self):
        for k in range(len(self.order)):
            for way in range(8):
                self.send(k, way).wait_send()


def gather_kernel(
    hidden_ref,
    gain_ref,
    router_ref,
    routes_ref,
    table_ref,
    kvw_ref,
    qw_ref,
    q_ref,
    gates_ref,
    tables_ref,
    gathered_ref,
    x_ref,
    weights,
    own_kv,
    send_sem,
    recv_sem,
    local_sem,
):
    kinds, experts = kvw_ref.shape[0], qw_ref.shape[0]

    def weight(c):
        own = kvw_ref.at[c] if c < kinds else qw_ref.at[c - kinds]
        return (own, lambda shard: weights.at[c, shard])

    def pair(c):
        return (own_kv.at[c], lambda shard: gathered_ref.at[shard, c])

    table = (table_ref, lambda shard: tables_ref.at[shard])
    early = min(2, experts)
    labels = [("w", c) for c in range(kinds)] + [("table", 0)]
    labels += [("w", c) for c in range(kinds, kinds + early)]
    labels += [("kv", c) for c in range(kinds)]
    labels += [("w", c) for c in range(kinds + early, kinds + experts)]
    order = [table if n == "table" else weight(c) if n == "w" else pair(c) for n, c in labels]
    ring = TokRing(order, send_sem, recv_sem, local_sem)
    ring.greet()

    def normalise():
        values = hidden_ref[...].astype(jnp.float32)
        factor = lax.rsqrt(jnp.mean(values * values, axis=-1, keepdims=True) + EPSILON)
        x_ref[...] = (values * factor * gain_ref[...]).astype(jnp.bfloat16)

    def gate():
        logits = jnp.dot(
            x_ref[...].astype(jnp.float32),
            router_ref[...],
            precision=lax.Precision.HIGHEST,
            preferred_element_type=jnp.float32,
        )
        ids = lax.broadcasted_iota(jnp.int32, logits.shape, 1)
        picked = [routes_ref[:, s : s + 1] == ids for s in range(routes_ref.shape[1])]
        chosen = [jnp.sum(jnp.where(p, logits, 0.0), axis=1, keepdims=True) for p in picked]
        top = functools.reduce(jnp.maximum, chosen)
        expon = [jnp.exp(c - top) for c in chosen]
        total = functools.reduce(jnp.add, expon)
        result = jnp.zeros_like(logits)
        for p, e in zip(picked, expon):
            result = jnp.where(p, e / total, result)
        gates_ref[...] = result

    def finish(k):
        kind, c = labels[k]
        if kind != "w":
            return
        depth = weights.shape[1] * weights.shape[2]
        w = weights[c].reshape(depth, weights.shape[3])
        y = jnp.dot(x_ref[...], w, preferred_element_type=jnp.float32).astype(jnp.bfloat16)
        if c < kinds:
            own_kv[c] = y
            return
        expert = c - kinds
        for s in range(q_ref.shape[0]):
            mine = routes_ref[:, s : s + 1] == expert
            before = jnp.zeros_like(y) if expert == 0 else q_ref[s]
            q_ref[s] = jnp.where(mine, y, before)

    for k in range(len(order) + 3):
        ring.step(k, finish)
        if k == 0:
            normalise()
        if k == 6:
            gate()
    ring.drain()


def gather_project(hidden, norm_gain, router_weight, routes, table, kv_weight, query_weight, shards):
    tokens, width = hidden.shape
    kinds, rows, cols = kv_weight.shape
    experts = query_weight.shape[0]
    slots = routes.shape[1]
    chunks = 2 * kinds + experts + 1
    vmem = pl.BlockSpec(memory_space=pltpu.VMEM)
    anywhere = pl.BlockSpec(memory_space=pl.ANY)
    return pl.pallas_call(
        gather_kernel,
        in_specs=[vmem, vmem, vmem, vmem, vmem, anywhere, anywhere],
        out_specs=[vmem, vmem, vmem, anywhere],
        out_shape=[
            jax.ShapeDtypeStruct((slots, tokens, cols), jnp.bfloat16),
            jax.ShapeDtypeStruct((tokens, experts), jnp.float32),
            jax.ShapeDtypeStruct((shards,) + table.shape, jnp.int32),
            jax.ShapeDtypeStruct((shards, kinds, tokens, cols), jnp.bfloat16),
        ],
        scratch_shapes=[
            pltpu.VMEM((tokens, width), jnp.bfloat16),
            pltpu.VMEM((kinds + experts, shards, rows, cols), jnp.bfloat16),
            pltpu.VMEM((kinds, tokens, cols), jnp.bfloat16),
            pltpu.SemaphoreType.DMA((chunks, 8)),
            pltpu.SemaphoreType.DMA((chunks, 8)),
            pltpu.SemaphoreType.DMA((chunks,)),
        ],
        compiler_params=pltpu.CompilerParams(
            collective_id=1, has_side_effects=True, vmem_limit_bytes=LARGE_VMEM_BYTES
        ),
        cost_estimate=pl.CostEstimate(
            flops=2 * (kinds + experts) * tokens * width * cols * 10,
            bytes_accessed=200 * 1024 * 1024,
            transcendentals=0,
        ),
        name="gather_project",
    )(hidden, norm_gain[None, :], router_weight, routes, table, kv_weight, query_weight)


def attend_gather_kernel(
    q_ref,
    lower_ref,
    kv_ref,
    ow_ref,
    out_ref,
    full_ref,
    held,
    load_sem,
    send_sem,
    recv_sem,
    local_sem,
    *,
    tile,
    block_k,
    heads,
    most,
):
    experts = ow_ref.shape[0]
    slots, tokens, cols = q_ref.shape
    shards = kv_ref.shape[0]
    load = pltpu.make_async_copy(kv_ref, held, load_sem)
    load.start()

    def chunk(e):
        return (ow_ref.at[e], lambda shard: full_ref.at[shard, e])

    ring = TokRing([chunk(e) for e in range(experts)], send_sem, recv_sem, local_sem)
    ring.greet()
    ring.step(0)
    columns = slots * tile
    per_shard = tokens // block_k

    def attend_tile(group, step):
        first = ring.me * tokens + step * tile
        begin = jnp.maximum(first + 1 - most, 0) // block_k
        inner = (first + 1) // block_k
        end = (first + tile - 1) // block_k + 1
        lower = jnp.concatenate([lower_ref[step]] * slots, axis=1)
        q_pos = first + lax.broadcasted_iota(jnp.int32, (1, columns), 1) % tile
        spans = [slice((group * heads + h) * HDIM, (group * heads + h + 1) * HDIM) for h in range(heads)]
        rows_q = slice(step * tile, (step + 1) * tile)
        queries = [q_ref[:, rows_q, span].reshape(columns, HDIM) for span in spans]

        def body(block, carry, causal):
            shard = block // per_shard
            rows = pl.ds((block % per_shard) * block_k, block_k)
            k_pos = block * block_k + lax.broadcasted_iota(jnp.int32, (block_k, columns), 0)
            allowed = k_pos >= lower
            if causal:
                allowed = allowed & (k_pos <= q_pos)
            result = []
            for h in range(heads):
                peak, total, accum = carry[h]
                keys = held[shard, 0, rows, spans[h]]
                values = held[shard, 1, rows, spans[h]]
                scores = lax.dot_general(
                    keys, queries[h], (((1,), (1,)), ((), ())), preferred_element_type=jnp.float32
                ) * SCALE
                scores = jnp.where(allowed, scores, MASKED)
                new_peak = jnp.maximum(peak, jnp.max(scores, axis=0, keepdims=True))
                expon = jnp.exp2(scores - new_peak)
                shrink = jnp.exp2(peak - new_peak)
                total = total * shrink + jnp.sum(expon, axis=0, keepdims=True)
                accum = accum * shrink + lax.dot_general(
                    values,
                    expon.astype(jnp.bfloat16),
                    (((0,), (0,)), ((), ())),
                    preferred_element_type=jnp.float32,
                )
                result.append((new_peak, total, accum))
            return tuple(result)

        state = tuple(
            (
                jnp.full((1, columns), MASKED, jnp.float32),
                jnp.zeros((1, columns), jnp.float32),
                jnp.zeros((HDIM, columns), jnp.float32),
            )
            for _ in range(heads)
        )
        state = lax.fori_loop(begin, inner, functools.partial(body, causal=False), state)
        state = lax.fori_loop(inner, end, functools.partial(body, causal=True), state)
        for h in range(heads):
            _, total, accum = state[h]
            part = (accum / total).T.astype(jnp.bfloat16)
            out_ref[:, rows_q, spans[h]] = part.reshape(slots, tile, HDIM)

    ring.step(1)
    load.wait()
    work = [(g, t) for g in range(cols // (heads * HDIM)) for t in range(tokens // tile)]
    k = 2
    for group, step in work:
        attend_tile(group, step)
        if k < experts + 3:
            ring.step(k)
            k += 1
    for rest in range(k, experts + 3):
        ring.step(rest)
    ring.drain()


def attend_gather(queries, lower, key_values, out_weight, most):
    slots, tokens, cols = queries.shape
    shards = key_values.shape[0]
    experts, rows, out_cols = out_weight.shape
    heads = math.gcd(cols // HDIM, 2)
    tile = math.gcd(tokens, 256)
    vmem = pl.BlockSpec(memory_space=pltpu.VMEM)
    anywhere = pl.BlockSpec(memory_space=pl.ANY)
    return pl.pallas_call(
        functools.partial(
            attend_gather_kernel, tile=tile, block_k=math.gcd(tokens, 512), heads=heads, most=most
        ),
        in_specs=[vmem, vmem, anywhere, anywhere],
        out_specs=[vmem, anywhere],
        out_shape=[
            jax.ShapeDtypeStruct((slots, tokens, cols), jnp.bfloat16),
            jax.ShapeDtypeStruct((shards, experts, rows, out_cols), jnp.bfloat16),
        ],
        scratch_shapes=[
            pltpu.VMEM(key_values.shape, jnp.bfloat16),
            pltpu.SemaphoreType.DMA,
            pltpu.SemaphoreType.DMA((experts, 8)),
            pltpu.SemaphoreType.DMA((experts, 8)),
            pltpu.SemaphoreType.DMA((experts,)),
        ],
        compiler_params=pltpu.CompilerParams(
            collective_id=3, has_side_effects=True, vmem_limit_bytes=LARGE_VMEM_BYTES
        ),
        cost_estimate=pl.CostEstimate(
            flops=4 * slots * tokens * cols * most * 10,
            bytes_accessed=2 * (queries.size * 2 + key_values.size + 2 * shards * out_weight.size),
            transcendentals=slots * tokens * (cols // HDIM) * most,
        ),
        name="attend_gather",
    )(queries, lower.reshape(tokens // tile, 1, tile), key_values, out_weight)


def out_sum_kernel(
    x_ref,
    routes_ref,
    gates_ref,
    hidden_ref,
    w_ref,
    out_ref,
    weights,
    picked,
    own,
    near,
    far,
    load_sem,
    send_sem,
    recv_sem,
):
    me = lax.axis_index("mdl")
    low, high = me % 2, me // 2
    near_id, far_id = me + 1 - 2 * low, me + 2 - 4 * high
    both = near_id + 2 - 4 * high
    shards, experts = w_ref.shape[:2]
    cols = w_ref.shape[3]
    per = shards // 4
    targets = [both, near_id, far_id, me]

    def load(n):
        index = targets[n // per] * per + n % per
        return pltpu.make_async_copy(w_ref.at[index], weights.at[n], load_sem.at[n])

    for n in range(shards):
        load(n).start()

    barrier = pltpu.get_barrier_semaphore()
    for other in (near_id, far_id):
        pl.semaphore_signal(
            barrier, inc=1, device_id={"mdl": other}, device_id_type=pl.DeviceIdType.MESH
        )
    pl.semaphore_wait(barrier, 2)

    for e in range(experts):
        rows = jnp.zeros_like(x_ref[0])
        for s in range(x_ref.shape[0]):
            rows = jnp.where(routes_ref[:, s : s + 1] == e, x_ref[s], rows)
        picked[e] = rows

    def copy(way, src, dst, other):
        return pltpu.make_async_remote_copy(
            src_ref=src,
            dst_ref=dst,
            send_sem=send_sem.at[way],
            recv_sem=recv_sem.at[way],
            device_id={"mdl": other},
            device_id_type=pl.DeviceIdType.MESH,
        )

    def near_copy(way):
        return copy(way, own.at[way], near.at[way], near_id)

    def far_copy():
        return copy(2, own.at[2], far, far_id)

    def block(n, piece):
        load(n * per + piece).wait()
        total = jnp.zeros((own.shape[1], cols), jnp.float32)
        for e in range(experts):
            term = jnp.dot(picked[e], weights[n * per + piece, e], preferred_element_type=jnp.float32)
            total = total + gates_ref[:, e : e + 1] * term
        return total

    for n in range(4):
        for piece in range(per):
            span = slice(piece * cols, (piece + 1) * cols)
            own[n, :, span] = block(n, piece).astype(jnp.bfloat16)
        if n < 2:
            near_copy(n).start()
        elif n == 2:
            near_copy(0).wait_recv()
            own[2] = (own[2].astype(jnp.float32) + near[0].astype(jnp.float32)).astype(jnp.bfloat16)
            far_copy().start()
    near_copy(1).wait_recv()
    part = own[3].astype(jnp.float32) + near[1].astype(jnp.float32) + hidden_ref[...].astype(jnp.float32)
    far_copy().wait_recv()
    out_ref[...] = (part + far[...].astype(jnp.float32)).astype(jnp.bfloat16)
    near_copy(0).wait_send()
    near_copy(1).wait_send()
    far_copy().wait_send()


def project_out_sum(attended, routes, gates, residual, weight):
    shards, experts, rows, cols = weight.shape
    _, tokens, _ = attended.shape
    span = shards * cols // 4
    vmem = pl.BlockSpec(memory_space=pltpu.VMEM)
    return pl.pallas_call(
        out_sum_kernel,
        in_specs=[vmem, vmem, vmem, vmem, pl.BlockSpec(memory_space=pl.ANY)],
        out_specs=vmem,
        out_shape=jax.ShapeDtypeStruct((tokens, span), jnp.bfloat16),
        scratch_shapes=[
            pltpu.VMEM((shards, experts, rows, cols), jnp.bfloat16),
            pltpu.VMEM((experts, tokens, rows), jnp.bfloat16),
            pltpu.VMEM((4, tokens, span), jnp.bfloat16),
            pltpu.VMEM((2, tokens, span), jnp.bfloat16),
            pltpu.VMEM((tokens, span), jnp.bfloat16),
            pltpu.SemaphoreType.DMA((shards,)),
            pltpu.SemaphoreType.DMA((3,)),
            pltpu.SemaphoreType.DMA((3,)),
        ],
        compiler_params=pltpu.CompilerParams(
            collective_id=2, has_side_effects=True, vmem_limit_bytes=VMEM_BYTES
        ),
        cost_estimate=pl.CostEstimate(
            flops=2 * experts * tokens * rows * shards * cols,
            bytes_accessed=2 * weight.size,
            transcendentals=0,
        ),
        name="project_out_sum",
    )(attended, routes, gates, residual, weight)


def local(
    hidden,
    segment_ids,
    routes,
    norm_gain,
    router_weight,
    query_weight,
    kv_weight,
    out_weight,
    page_table,
):
    tok_dev, width = hidden.shape
    head_cols = query_weight.shape[2]
    shards = lax.axis_size("tok")
    parts = lax.axis_size("mdl")
    tok_row = lax.axis_index("tok")
    pages_here = page_table.shape[0]
    page_rows = tok_dev // pages_here

    own_kernels = shards == 8 and parts == 4
    if own_kernels:
        padded = jnp.zeros((16, 128), jnp.int32).at[0, :pages_here].set(page_table)
        queries, gates, tables, key_values = gather_project(
            hidden, norm_gain, router_weight, routes, padded, kv_weight, query_weight, shards
        )
        table = tables[:, 0, :pages_here].reshape(-1)
    else:
        table = lax.all_gather(page_table, "tok", axis=0, tiled=True)
        normed = rms_norm(hidden, norm_gain)
        gates = route_gates(normed, router_weight, routes)
        out_full = lax.all_gather(out_weight, "tok", axis=0)
        kv_full = lax.all_gather(kv_weight, "tok", axis=0)
        key_values = lax.all_gather(project_kv(normed, kv_full), "tok", axis=0)
        query_full = lax.all_gather(query_weight, "tok", axis=0)
        queries = project_queries(normed, routes, query_full)

    here = tok_row * pages_here + jnp.arange(pages_here, dtype=jnp.int32)
    logical = jnp.arange(table.shape[0], dtype=jnp.int32)
    source = jnp.sum(jnp.where(table[None, :] == here[:, None], logical[None, :], 0), axis=1)
    paged = key_values.reshape(shards, 2, pages_here, page_rows, head_cols)
    cache = paged[source // pages_here, :, source % pages_here].transpose(0, 2, 1, 3)

    prompt_ids = jnp.arange(SEGS, dtype=jnp.int32)
    seg_first = jnp.sum((segment_ids[:, None] < prompt_ids[None, :]).astype(jnp.int32), axis=0)
    first = (tok_row * tok_dev).astype(jnp.int32)
    own_seg = lax.dynamic_slice_in_dim(segment_ids, first, tok_dev, 0)
    lower = jnp.sum(
        jnp.where(own_seg[:, None] == prompt_ids[None, :], seg_first[None, :], 0), axis=1
    )

    span = width // parts
    residual = lax.dynamic_slice_in_dim(hidden, lax.axis_index("mdl") * span, span, 1)
    if own_kernels:
        most = segment_ids.shape[0] // 2
        attended, out_full = attend_gather(queries, lower, key_values, out_weight, most)
        return (project_out_sum(attended, routes, gates, residual, out_full), cache)
    attended = attend(queries, lower, key_values, first)
    partial_sums = project_out(attended, routes, gates, out_full, parts)
    mine = lax.psum_scatter(partial_sums, "mdl", scatter_dimension=0, tiled=False)
    output = (residual.astype(jnp.float32) + mine.astype(jnp.float32)).astype(jnp.bfloat16)
    return (output, cache)


def solution(mesh):
    placed = (
        P("tok", None),
        P(),
        P("tok", None),
        P(),
        P(),
        P(None, "tok", "mdl"),
        P(None, "tok", "mdl"),
        P(None, "mdl", "tok"),
        P("tok"),
    )
    return jax.shard_map(
        local,
        mesh=mesh,
        in_specs=placed,
        out_specs=(P("tok", "mdl"), P("tok", None, None, "mdl")),
        check_vma=False,
    )
```

```python
import functools
import math

import jax
import jax.numpy as jnp
from jax import lax
from jax.experimental import pallas as pl
from jax.experimental.pallas import tpu as pltpu
from jax.sharding import PartitionSpec as P

HDIM = 128
SEGS = 4
EPSILON = 1e-05
MASKED = -1e30
VMEM_BYTES = 48 * 1024 * 1024
LARGE_VMEM_BYTES = 60 * 1024 * 1024
SCALE = math.log2(math.e) / math.sqrt(HDIM)


def rms_norm(hidden, norm_gain):
    values = hidden.astype(jnp.float32)
    factor = lax.rsqrt(jnp.mean(values * values, axis=-1, keepdims=True) + EPSILON)
    return (values * factor * norm_gain).astype(jnp.bfloat16)


def route_gates(normed, router_weight, routes):
    logits = jnp.dot(normed.astype(jnp.float32), router_weight, precision=lax.Precision.HIGHEST)
    expert_ids = jnp.arange(logits.shape[1], dtype=jnp.int32)
    picked = routes[:, :, None] == expert_ids[None, None, :]
    chosen = jnp.sum(jnp.where(picked, logits[:, None, :], jnp.float32(0.0)), axis=-1)
    gates = jax.nn.softmax(chosen, axis=-1)
    return jnp.sum(jnp.where(picked, gates[:, :, None], jnp.float32(0.0)), axis=1)


def params():
    return pltpu.CompilerParams(
        dimension_semantics=("arbitrary",), vmem_limit_bytes=VMEM_BYTES
    )


def kv_kernel(x_ref, w_ref, out_ref):
    depth = w_ref.shape[0] * w_ref.shape[2]
    w = w_ref[:, 0].reshape(depth, w_ref.shape[3])
    out_ref[0] = jnp.dot(x_ref[...], w, preferred_element_type=jnp.float32).astype(jnp.bfloat16)


def project_kv(normed, weight):
    shards, kinds, rows, cols = weight.shape
    tokens, width = normed.shape
    return pl.pallas_call(
        kv_kernel,
        grid=(kinds,),
        in_specs=[
            pl.BlockSpec((tokens, width), lambda c: (0, 0)),
            pl.BlockSpec((shards, 1, rows, cols), lambda c: (0, c, 0, 0)),
        ],
        out_specs=pl.BlockSpec((1, tokens, cols), lambda c: (c, 0, 0)),
        out_shape=jax.ShapeDtypeStruct((kinds, tokens, cols), jnp.bfloat16),
        compiler_params=params(),
        cost_estimate=pl.CostEstimate(
            flops=2 * kinds * tokens * width * cols,
            bytes_accessed=2 * (weight.size + normed.size + kinds * tokens * cols),
            transcendentals=0,
        ),
        name="project_kv",
    )(normed, weight)


def query_kernel(x_ref, routes_ref, w_ref, out_ref):
    expert = pl.program_id(0)
    depth = w_ref.shape[0] * w_ref.shape[2]
    w = w_ref[:, 0].reshape(depth, w_ref.shape[3])
    y = jnp.dot(x_ref[...], w, preferred_element_type=jnp.float32).astype(jnp.bfloat16)

    @pl.when(expert == 0)
    def _():
        out_ref[...] = jnp.zeros_like(out_ref)

    for slot in range(out_ref.shape[0]):
        mine = routes_ref[:, slot : slot + 1] == expert
        out_ref[slot] = jnp.where(mine, y, out_ref[slot])


def project_queries(normed, routes, weight):
    shards, experts, rows, cols = weight.shape
    tokens, width = normed.shape
    slots = routes.shape[1]
    return pl.pallas_call(
        query_kernel,
        grid=(experts,),
        in_specs=[
            pl.BlockSpec((tokens, width), lambda e: (0, 0)),
            pl.BlockSpec((tokens, slots), lambda e: (0, 0)),
            pl.BlockSpec((shards, 1, rows, cols), lambda e: (0, e, 0, 0)),
        ],
        out_specs=pl.BlockSpec((slots, tokens, cols), lambda e: (0, 0, 0)),
        out_shape=jax.ShapeDtypeStruct((slots, tokens, cols), jnp.bfloat16),
        compiler_params=params(),
        cost_estimate=pl.CostEstimate(
            flops=2 * experts * tokens * width * cols,
            bytes_accessed=2 * (weight.size + normed.size + slots * tokens * cols),
            transcendentals=0,
        ),
        name="project_queries",
    )(normed, routes, weight)


def attention_kernel(bounds_ref, q_ref, lower_ref, kv_ref, out_ref, *, block_k, heads, tile):
    pos_first = bounds_ref[0]
    step = pl.program_id(1)
    first = pos_first + step * tile
    low = bounds_ref[1 + 2 * step]
    high = bounds_ref[2 + 2 * step]
    slots = q_ref.shape[0]
    columns = slots * tile
    per_shard = kv_ref.shape[2] // block_k
    begin = low // block_k
    end = (first + tile - 1) // block_k + 1
    q_pos = first + lax.broadcasted_iota(jnp.int32, (1, columns), 1) % tile
    lower = jnp.concatenate([lower_ref[0]] * slots, axis=1)
    queries = [
        q_ref[:, :, h * HDIM : (h + 1) * HDIM].reshape(columns, HDIM) for h in range(heads)
    ]

    def body(block, carry, masked):
        shard = block // per_shard
        rows = pl.ds((block % per_shard) * block_k, block_k)
        if masked:
            k_pos = block * block_k + lax.broadcasted_iota(jnp.int32, (block_k, columns), 0)
            allowed = (k_pos >= lower) & (k_pos <= q_pos)
        result = []
        for h in range(heads):
            peak, total, accum = carry[h]
            span = slice(h * HDIM, (h + 1) * HDIM)
            keys = kv_ref[shard, 0, rows, span]
            values = kv_ref[shard, 1, rows, span]
            scores = lax.dot_general(
                keys, queries[h], (((1,), (1,)), ((), ())), preferred_element_type=jnp.float32
            ) * SCALE
            if masked:
                scores = jnp.where(allowed, scores, MASKED)
            new_peak = jnp.maximum(peak, jnp.max(scores, axis=0, keepdims=True))
            expon = jnp.exp2(scores - new_peak)
            if masked:
                expon = jnp.where(allowed, expon, 0.0)
            shrink = jnp.exp2(peak - new_peak)
            total = total * shrink + jnp.sum(expon, axis=0, keepdims=True)
            accum = accum * shrink + lax.dot_general(
                values,
                expon.astype(jnp.bfloat16),
                (((0,), (0,)), ((), ())),
                preferred_element_type=jnp.float32,
            )
            result.append((new_peak, total, accum))
        return tuple(result)

    state = tuple(
        (
            jnp.full((1, columns), MASKED, jnp.float32),
            jnp.zeros((1, columns), jnp.float32),
            jnp.zeros((HDIM, columns), jnp.float32),
        )
        for _ in range(heads)
    )
    inner = jnp.maximum((first + 1) // block_k, begin)
    clear = jnp.clip((high + block_k - 1) // block_k, begin, inner)
    state = lax.fori_loop(begin, clear, functools.partial(body, masked=True), state)
    state = lax.fori_loop(clear, inner, functools.partial(body, masked=False), state)
    state = lax.fori_loop(inner, end, functools.partial(body, masked=True), state)
    for h in range(heads):
        _, total, accum = state[h]
        rows = (accum / total).T.astype(jnp.bfloat16)
        out_ref[:, :, h * HDIM : (h + 1) * HDIM] = rows.reshape(slots, tile, HDIM)


def attend(queries, lower, key_values, first):
    slots, tokens, cols = queries.shape
    shards, kinds, rows, _ = key_values.shape
    heads = math.gcd(cols // HDIM, 2)
    tile = math.gcd(tokens, 256)
    block_k = math.gcd(rows, 512)
    by_tile = lower.reshape(tokens // tile, tile)
    bounds = jnp.concatenate(
        [first[None], jnp.stack([by_tile[:, 0], by_tile[:, -1]], axis=1).reshape(-1)]
    ).astype(jnp.int32)
    return pl.pallas_call(
        functools.partial(attention_kernel, block_k=block_k, heads=heads, tile=tile),
        grid=(cols // (heads * HDIM), tokens // tile),
        in_specs=[
            pl.BlockSpec(memory_space=pltpu.SMEM),
            pl.BlockSpec((slots, tile, heads * HDIM), lambda g, t: (0, t, g)),
            pl.BlockSpec((1, 1, tile), lambda g, t: (t, 0, 0)),
            pl.BlockSpec((shards, kinds, rows, heads * HDIM), lambda g, t: (0, 0, 0, g)),
        ],
        out_specs=pl.BlockSpec((slots, tile, heads * HDIM), lambda g, t: (0, t, g)),
        out_shape=jax.ShapeDtypeStruct((slots, tokens, cols), jnp.bfloat16),
        compiler_params=pltpu.CompilerParams(
            dimension_semantics=("arbitrary", "arbitrary"), vmem_limit_bytes=VMEM_BYTES
        ),
        cost_estimate=pl.CostEstimate(
            flops=4 * slots * tokens * cols * 2048,
            bytes_accessed=2 * (queries.size * 2 + key_values.size),
            transcendentals=slots * tokens * (cols // HDIM) * 2048,
        ),
        name="attend",
    )(bounds, queries, by_tile[:, None, :], key_values)


def out_kernel(x_ref, routes_ref, gates_ref, w_ref, out_ref, picked):
    experts = w_ref.shape[1]

    @pl.when(pl.program_id(0) == 0)
    def _():
        for e in range(experts):
            rows = jnp.zeros_like(x_ref[0])
            for slot in range(x_ref.shape[0]):
                rows = jnp.where(routes_ref[:, slot : slot + 1] == e, x_ref[slot], rows)
            picked[e] = rows

    total = jnp.zeros(out_ref.shape[1:], jnp.float32)
    for e in range(experts):
        term = jnp.dot(picked[e], w_ref[0, e], preferred_element_type=jnp.float32)
        total = total + gates_ref[:, e : e + 1] * term
    out_ref[0] = total.astype(jnp.bfloat16)


def project_out(attended, routes, gates, weight, parts):
    shards, experts, rows, cols = weight.shape
    slots, tokens, _ = attended.shape
    span = shards * cols // parts
    per = span // cols
    return pl.pallas_call(
        out_kernel,
        grid=(shards,),
        in_specs=[
            pl.BlockSpec((slots, tokens, rows), lambda i: (0, 0, 0)),
            pl.BlockSpec((tokens, slots), lambda i: (0, 0)),
            pl.BlockSpec((tokens, experts), lambda i: (0, 0)),
            pl.BlockSpec((1, experts, rows, cols), lambda i: (i, 0, 0, 0)),
        ],
        out_specs=pl.BlockSpec((1, tokens, cols), lambda i: (i // per, 0, i % per)),
        out_shape=jax.ShapeDtypeStruct((parts, tokens, span), jnp.bfloat16),
        scratch_shapes=[pltpu.VMEM((experts, tokens, rows), jnp.bfloat16)],
        compiler_params=params(),
        cost_estimate=pl.CostEstimate(
            flops=2 * experts * tokens * rows * shards * cols,
            bytes_accessed=2 * (weight.size + attended.size + tokens * shards * cols),
            transcendentals=0,
        ),
        name="project_out",
    )(attended, routes, gates, weight)


class TokRing:
    def __init__(self, order, send_sem, recv_sem, local_sem, lag):
        self.lag = lag
        me = lax.axis_index("tok")
        core, col, row = me % 2, (me // 2) % 2, me // 4
        to_core, to_col, to_row = 1 - 2 * core, 2 - 4 * col, 4 - 8 * row
        self.me, self.to_core = me, to_core
        self.mate, self.side, self.over = me + to_core, me + to_col, me + to_row
        self.across = me + to_col + to_row
        self.order = order
        self.send_sem, self.recv_sem, self.local_sem = send_sem, recv_sem, local_sem

    def greet(self, along_mdl=()):
        barrier = pltpu.get_barrier_semaphore()
        for other in along_mdl:
            pl.semaphore_signal(
                barrier, inc=1, device_id={"mdl": other}, device_id_type=pl.DeviceIdType.MESH
            )
        for other in (self.mate, self.side, self.over):
            pl.semaphore_signal(
                barrier, inc=1, device_id={"tok": other}, device_id_type=pl.DeviceIdType.MESH
            )
        pl.semaphore_wait(barrier, 3 + len(along_mdl))

    def half(self, ref, part):
        rows = ref.shape[0] // 2
        return ref.at[pl.ds(part * rows, rows)]

    def copy(self, k, way, src, dst, other):
        return pltpu.make_async_remote_copy(
            src_ref=src,
            dst_ref=dst,
            send_sem=self.send_sem.at[k, way],
            recv_sem=self.recv_sem.at[k, way],
            device_id={"tok": other},
            device_id_type=pl.DeviceIdType.MESH,
        )

    def send(self, k, way):
        own, slot = self.order[k]
        if way < 3:
            return self.copy(k, way, own, slot(self.me), (self.mate, self.side, self.over)[way])
        place, other = [
            lambda: (self.half(slot(self.over), 0), self.side),
            lambda: (self.half(slot(self.side), 1), self.over),
            lambda: (slot(self.side), self.mate),
            lambda: (slot(self.over), self.mate),
            lambda: (slot(self.across), self.mate),
        ][way - 3]()
        return self.copy(k, way, place, place, other)

    def arrival(self, k, way):
        slot = self.order[k][1]
        place = [
            lambda: slot(self.mate),
            lambda: slot(self.side),
            lambda: slot(self.over),
            lambda: self.half(slot(self.across), 0),
            lambda: self.half(slot(self.across), 1),
            lambda: slot(self.side + self.to_core),
            lambda: slot(self.over + self.to_core),
            lambda: slot(self.across + self.to_core),
        ][way]()
        return self.copy(k, way, place, place, self.mate)

    def keep(self, k):
        own, slot = self.order[k]
        return pltpu.make_async_copy(own, slot(self.me), self.local_sem.at[k])

    def begin(self, k):
        for way in (1, 2, 0):
            self.send(k, way).start()
        self.keep(k).start()

    def forward(self, k):
        self.arrival(k, 1).wait_recv()
        self.send(k, 4).start()
        self.send(k, 5).start()
        self.arrival(k, 2).wait_recv()
        self.send(k, 3).start()
        self.send(k, 6).start()

    def share(self, k):
        self.arrival(k, 3).wait_recv()
        self.arrival(k, 4).wait_recv()
        self.send(k, 7).start()

    def complete(self, k):
        for way in (0, 5, 6, 7):
            self.arrival(k, way).wait_recv()
        self.keep(k).wait()

    def step(self, k, finish=None):
        count = len(self.order)
        if k < count:
            self.begin(k)
        j = k - self.lag
        if 0 <= j < count:
            self.forward(j)
        if 0 <= j - 1 < count:
            self.share(j - 1)
        if 0 <= j - 2 < count:
            self.complete(j - 2)
            if finish is not None:
                finish(j - 2)

    def drain(self):
        for k in range(len(self.order)):
            for way in range(8):
                self.send(k, way).wait_send()


def gather_kernel(
    hidden_ref,
    gain_ref,
    router_ref,
    routes_ref,
    table_ref,
    kvw_ref,
    qw_ref,
    q_ref,
    gates_ref,
    tables_ref,
    gathered_ref,
    x_ref,
    weights,
    own_kv,
    send_sem,
    recv_sem,
    local_sem,
):
    kinds, experts = kvw_ref.shape[0], qw_ref.shape[0]

    def weight(c):
        own = kvw_ref.at[c] if c < kinds else qw_ref.at[c - kinds]
        return (own, lambda shard: weights.at[c, shard])

    def pair(c):
        return (own_kv.at[c], lambda shard: gathered_ref.at[shard, c])

    table = (table_ref, lambda shard: tables_ref.at[shard])
    early = min(2, experts)
    labels = [("w", c) for c in range(kinds)] + [("table", 0)]
    labels += [("w", c) for c in range(kinds, kinds + early)]
    labels += [("kv", c) for c in range(kinds)]
    labels += [("w", c) for c in range(kinds + early, kinds + experts)]
    order = [table if n == "table" else weight(c) if n == "w" else pair(c) for n, c in labels]
    ring = TokRing(order, send_sem, recv_sem, local_sem, 1)
    ring.greet()

    def normalise():
        values = hidden_ref[...].astype(jnp.float32)
        factor = lax.rsqrt(jnp.mean(values * values, axis=-1, keepdims=True) + EPSILON)
        x_ref[...] = (values * factor * gain_ref[...]).astype(jnp.bfloat16)

    def gate():
        logits = lax.dot_general(
            x_ref[...].astype(jnp.float32),
            router_ref[...],
            (((1,), (1,)), ((), ())),
            precision=lax.Precision.HIGHEST,
            preferred_element_type=jnp.float32,
        )
        ids = lax.broadcasted_iota(jnp.int32, logits.shape, 1)
        picked = [routes_ref[:, s : s + 1] == ids for s in range(routes_ref.shape[1])]
        chosen = [jnp.sum(jnp.where(p, logits, 0.0), axis=1, keepdims=True) for p in picked]
        top = functools.reduce(jnp.maximum, chosen)
        expon = [jnp.exp(c - top) for c in chosen]
        total = functools.reduce(jnp.add, expon)
        result = jnp.zeros_like(logits)
        for p, e in zip(picked, expon):
            result = jnp.where(p, e / total, result)
        gates_ref[...] = result

    def finish(k):
        kind, c = labels[k]
        if kind != "w":
            return
        depth = weights.shape[1] * weights.shape[2]
        w = weights[c].reshape(depth, weights.shape[3])
        y = jnp.dot(x_ref[...], w, preferred_element_type=jnp.float32).astype(jnp.bfloat16)
        if c < kinds:
            own_kv[c] = y
            return
        expert = c - kinds
        for s in range(q_ref.shape[0]):
            mine = routes_ref[:, s : s + 1] == expert
            before = jnp.zeros_like(y) if expert == 0 else q_ref[s]
            q_ref[s] = jnp.where(mine, y, before)

    for k in range(len(order) + 3):
        ring.step(k, finish)
        if k == 0:
            normalise()
        if k == 6:
            gate()
    ring.drain()


def gather_project(hidden, norm_gain, router_weight, routes, table, kv_weight, query_weight, shards):
    tokens, width = hidden.shape
    kinds, rows, cols = kv_weight.shape
    experts = query_weight.shape[0]
    slots = routes.shape[1]
    chunks = 2 * kinds + experts + 1
    vmem = pl.BlockSpec(memory_space=pltpu.VMEM)
    anywhere = pl.BlockSpec(memory_space=pl.ANY)
    return pl.pallas_call(
        gather_kernel,
        in_specs=[vmem, vmem, vmem, vmem, vmem, anywhere, anywhere],
        out_specs=[vmem, vmem, vmem, anywhere],
        out_shape=[
            jax.ShapeDtypeStruct((slots, tokens, cols), jnp.bfloat16),
            jax.ShapeDtypeStruct((tokens, experts), jnp.float32),
            jax.ShapeDtypeStruct((shards,) + table.shape, jnp.int32),
            jax.ShapeDtypeStruct((shards, kinds, tokens, cols), jnp.bfloat16),
        ],
        scratch_shapes=[
            pltpu.VMEM((tokens, width), jnp.bfloat16),
            pltpu.VMEM((kinds + experts, shards, rows, cols), jnp.bfloat16),
            pltpu.VMEM((kinds, tokens, cols), jnp.bfloat16),
            pltpu.SemaphoreType.DMA((chunks, 8)),
            pltpu.SemaphoreType.DMA((chunks, 8)),
            pltpu.SemaphoreType.DMA((chunks,)),
        ],
        compiler_params=pltpu.CompilerParams(
            collective_id=1, has_side_effects=True, vmem_limit_bytes=LARGE_VMEM_BYTES
        ),
        cost_estimate=pl.CostEstimate(
            flops=2 * (kinds + experts) * tokens * width * cols * 10,
            bytes_accessed=200 * 1024 * 1024,
            transcendentals=0,
        ),
        name="gather_project",
    )(hidden, norm_gain[None, :], router_weight.T, routes, table, kv_weight, query_weight)


def attend_out_kernel(
    q_ref,
    lower_ref,
    routes_ref,
    gates_ref,
    residual_ref,
    kv_ref,
    ow_ref,
    out_ref,
    held,
    attended,
    weights,
    picked,
    own,
    near,
    far,
    load_sem,
    send_sem,
    recv_sem,
    local_sem,
    sum_send_sem,
    sum_recv_sem,
    *,
    tile,
    block_k,
    heads,
    most,
):
    experts = ow_ref.shape[0]
    slots, tokens, cols = q_ref.shape
    shards = kv_ref.shape[0]
    halves, lanes = weights.shape[0], weights.shape[4]
    per = shards // 4
    mdl = lax.axis_index("mdl")
    low, high = mdl % 2, mdl // 2
    near_id, far_id = mdl + 1 - 2 * low, mdl + 2 - 4 * high
    targets = [near_id + 2 - 4 * high, near_id, far_id, mdl]
    load = pltpu.make_async_copy(kv_ref, held, load_sem)
    load.start()

    def chunk(h, e):
        return (ow_ref.at[e, :, pl.ds(h * lanes, lanes)], lambda shard: weights.at[h, shard, e])

    order = [chunk(h, e) for h in range(halves) for e in range(experts)]
    ring = TokRing(order, send_sem, recv_sem, local_sem, 2)
    ring.greet((near_id, far_id))
    ring.step(0)
    ring.step(1)
    columns = slots * tile
    per_shard = tokens // block_k

    def attend_tile(group, step):
        first = ring.me * tokens + step * tile
        begin = jnp.maximum(first + 1 - most, 0) // block_k
        inner = (first + 1) // block_k
        end = (first + tile - 1) // block_k + 1
        lower = jnp.concatenate([lower_ref[step]] * slots, axis=1)
        q_pos = first + lax.broadcasted_iota(jnp.int32, (1, columns), 1) % tile
        spans = [slice((group * heads + h) * HDIM, (group * heads + h + 1) * HDIM) for h in range(heads)]
        rows_q = slice(step * tile, (step + 1) * tile)
        queries = [q_ref[:, rows_q, span].reshape(columns, HDIM) for span in spans]

        def body(block, carry, causal):
            shard = block // per_shard
            rows = pl.ds((block % per_shard) * block_k, block_k)
            k_pos = block * block_k + lax.broadcasted_iota(jnp.int32, (block_k, columns), 0)
            allowed = k_pos >= lower
            if causal:
                allowed = allowed & (k_pos <= q_pos)
            result = []
            for h in range(heads):
                peak, total, accum = carry[h]
                keys = held[shard, 0, rows, spans[h]]
                values = held[shard, 1, rows, spans[h]]
                scores = lax.dot_general(
                    keys, queries[h], (((1,), (1,)), ((), ())), preferred_element_type=jnp.float32
                ) * SCALE
                scores = jnp.where(allowed, scores, MASKED)
                new_peak = jnp.maximum(peak, jnp.max(scores, axis=0, keepdims=True))
                expon = jnp.exp2(scores - new_peak)
                shrink = jnp.exp2(peak - new_peak)
                total = total * shrink + jnp.sum(expon, axis=0, keepdims=True)
                accum = accum * shrink + lax.dot_general(
                    values,
                    expon.astype(jnp.bfloat16),
                    (((0,), (0,)), ((), ())),
                    preferred_element_type=jnp.float32,
                )
                result.append((new_peak, total, accum))
            return tuple(result)

        state = tuple(
            (
                jnp.full((1, columns), MASKED, jnp.float32),
                jnp.zeros((1, columns), jnp.float32),
                jnp.zeros((HDIM, columns), jnp.float32),
            )
            for _ in range(heads)
        )
        state = lax.fori_loop(begin, inner, functools.partial(body, causal=False), state)
        state = lax.fori_loop(inner, end, functools.partial(body, causal=True), state)
        for h in range(heads):
            _, total, accum = state[h]
            part = (accum / total).T.astype(jnp.bfloat16)
            attended[:, rows_q, spans[h]] = part.reshape(slots, tile, HDIM)

    def sum_copy(way, src, dst, other):
        return pltpu.make_async_remote_copy(
            src_ref=src,
            dst_ref=dst,
            send_sem=sum_send_sem.at[way],
            recv_sem=sum_recv_sem.at[way],
            device_id={"mdl": other},
            device_id_type=pl.DeviceIdType.MESH,
        )

    def near_copy(h, n):
        return sum_copy(3 * h + n, own.at[h, n], near.at[h, n], near_id)

    def far_copy(h):
        return sum_copy(3 * h + 2, own.at[h, 2], far.at[h], far_id)

    def block(h, n):
        total = jnp.zeros(own.shape[2:], jnp.float32)
        for e in range(experts):
            w = jnp.concatenate([weights[h, targets[n] * per + s, e] for s in range(per)], axis=1)
            term = jnp.dot(picked[e], w, preferred_element_type=jnp.float32)
            total = total + gates_ref[:, e : e + 1] * term
        own[h, n] = total.astype(jnp.bfloat16)

    def pass_on(h):
        near_copy(h, 0).wait_recv()
        both = own[h, 2].astype(jnp.float32) + near[h, 0].astype(jnp.float32)
        own[h, 2] = both.astype(jnp.bfloat16)
        far_copy(h).start()

    def close(h):
        near_copy(h, 1).wait_recv()
        far_copy(h).wait_recv()
        mine = own[h, 3].astype(jnp.float32) + near[h, 1].astype(jnp.float32)
        mine = mine + far[h].astype(jnp.float32)
        for s in range(per):
            at = slice((s * halves + h) * lanes, (s * halves + h + 1) * lanes)
            part = residual_ref[:, at].astype(jnp.float32) + mine[:, s * lanes : (s + 1) * lanes]
            out_ref[:, at] = part.astype(jnp.bfloat16)

    load.wait()
    k = 2
    for group in range(cols // (heads * HDIM)):
        for step in range(tokens // tile):
            attend_tile(group, step)
            ring.step(k)
            ring.step(k + 1)
            k += 2
    for e in range(experts):
        rows = jnp.zeros_like(attended[0])
        for s in range(slots):
            rows = jnp.where(routes_ref[:, s : s + 1] == e, attended[s], rows)
        picked[e] = rows
    last = len(order) + ring.lag + 2
    for h in range(halves):
        ready = (h + 1) * experts + ring.lag + 2
        for rest in range(k, ready):
            ring.step(rest)
        k = max(k, ready)
        for n in range(4):
            block(h, n)
            if n < 2:
                near_copy(h, n).start()
            if h + 1 < halves and k < last - 2:
                ring.step(k)
                k += 1
        pass_on(h)
    for h in range(halves):
        close(h)
    ring.drain()
    for h in range(halves):
        near_copy(h, 0).wait_send()
        near_copy(h, 1).wait_send()
        far_copy(h).wait_send()


def attend_out(queries, lower, routes, gates, residual, key_values, out_weight, most):
    slots, tokens, cols = queries.shape
    shards = key_values.shape[0]
    experts, rows, out_cols = out_weight.shape
    heads = math.gcd(cols // HDIM, 2)
    tile = math.gcd(tokens, 256)
    halves = 2
    lanes = out_cols // halves
    width = shards // 4 * lanes
    vmem = pl.BlockSpec(memory_space=pltpu.VMEM)
    anywhere = pl.BlockSpec(memory_space=pl.ANY)
    return pl.pallas_call(
        functools.partial(
            attend_out_kernel, tile=tile, block_k=math.gcd(tokens, 512), heads=heads, most=most
        ),
        in_specs=[vmem] * 5 + [anywhere] * 2,
        out_specs=vmem,
        out_shape=jax.ShapeDtypeStruct(residual.shape, jnp.bfloat16),
        scratch_shapes=[
            pltpu.VMEM(key_values.shape, jnp.bfloat16),
            pltpu.VMEM((slots, tokens, cols), jnp.bfloat16),
            pltpu.VMEM((halves, shards, experts, rows, lanes), jnp.bfloat16),
            pltpu.VMEM((experts, tokens, rows), jnp.bfloat16),
            pltpu.VMEM((halves, 4, tokens, width), jnp.bfloat16),
            pltpu.VMEM((halves, 2, tokens, width), jnp.bfloat16),
            pltpu.VMEM((halves, tokens, width), jnp.bfloat16),
            pltpu.SemaphoreType.DMA,
            pltpu.SemaphoreType.DMA((halves * experts, 8)),
            pltpu.SemaphoreType.DMA((halves * experts, 8)),
            pltpu.SemaphoreType.DMA((halves * experts,)),
            pltpu.SemaphoreType.DMA((3 * halves,)),
            pltpu.SemaphoreType.DMA((3 * halves,)),
        ],
        compiler_params=pltpu.CompilerParams(
            collective_id=3, has_side_effects=True, vmem_limit_bytes=LARGE_VMEM_BYTES
        ),
        cost_estimate=pl.CostEstimate(
            flops=4 * slots * tokens * cols * most * 10,
            bytes_accessed=2 * (queries.size * 2 + key_values.size + 2 * shards * out_weight.size),
            transcendentals=slots * tokens * (cols // HDIM) * most,
        ),
        name="attend_out",
    )(
        queries,
        lower.reshape(tokens // tile, 1, tile),
        routes,
        gates,
        residual,
        key_values,
        out_weight,
    )


def local(
    hidden,
    segment_ids,
    routes,
    norm_gain,
    router_weight,
    query_weight,
    kv_weight,
    out_weight,
    page_table,
):
    tok_dev, width = hidden.shape
    head_cols = query_weight.shape[2]
    shards = lax.axis_size("tok")
    parts = lax.axis_size("mdl")
    tok_row = lax.axis_index("tok")
    pages_here = page_table.shape[0]
    page_rows = tok_dev // pages_here

    own_kernels = shards == 8 and parts == 4
    if own_kernels:
        padded = jnp.zeros((16, 128), jnp.int32).at[0, :pages_here].set(page_table)
        queries, gates, tables, key_values = gather_project(
            hidden, norm_gain, router_weight, routes, padded, kv_weight, query_weight, shards
        )
        table = tables[:, 0, :pages_here].reshape(-1)
    else:
        table = lax.all_gather(page_table, "tok", axis=0, tiled=True)
        normed = rms_norm(hidden, norm_gain)
        gates = route_gates(normed, router_weight, routes)
        out_full = lax.all_gather(out_weight, "tok", axis=0)
        kv_full = lax.all_gather(kv_weight, "tok", axis=0)
        key_values = lax.all_gather(project_kv(normed, kv_full), "tok", axis=0)
        query_full = lax.all_gather(query_weight, "tok", axis=0)
        queries = project_queries(normed, routes, query_full)

    here = tok_row * pages_here + jnp.arange(pages_here, dtype=jnp.int32)
    logical = jnp.arange(table.shape[0], dtype=jnp.int32)
    source = jnp.sum(jnp.where(table[None, :] == here[:, None], logical[None, :], 0), axis=1)
    paged = key_values.reshape(shards, 2, pages_here, page_rows, head_cols)
    cache = paged[source // pages_here, :, source % pages_here].transpose(0, 2, 1, 3)

    prompt_ids = jnp.arange(SEGS, dtype=jnp.int32)
    seg_first = jnp.sum((segment_ids[:, None] < prompt_ids[None, :]).astype(jnp.int32), axis=0)
    first = (tok_row * tok_dev).astype(jnp.int32)
    own_seg = lax.dynamic_slice_in_dim(segment_ids, first, tok_dev, 0)
    lower = jnp.sum(
        jnp.where(own_seg[:, None] == prompt_ids[None, :], seg_first[None, :], 0), axis=1
    )

    span = width // parts
    residual = lax.dynamic_slice_in_dim(hidden, lax.axis_index("mdl") * span, span, 1)
    if own_kernels:
        most = segment_ids.shape[0] // 2
        args = (queries, lower, routes, gates, residual, key_values, out_weight, most)
        return (attend_out(*args), cache)
    attended = attend(queries, lower, key_values, first)
    partial_sums = project_out(attended, routes, gates, out_full, parts)
    mine = lax.psum_scatter(partial_sums, "mdl", scatter_dimension=0, tiled=False)
    output = (residual.astype(jnp.float32) + mine.astype(jnp.float32)).astype(jnp.bfloat16)
    return (output, cache)


def solution(mesh):
    placed = (
        P("tok", None),
        P(),
        P("tok", None),
        P(),
        P(),
        P(None, "tok", "mdl"),
        P(None, "tok", "mdl"),
        P(None, "mdl", "tok"),
        P("tok"),
    )
    return jax.shard_map(
        local,
        mesh=mesh,
        in_specs=placed,
        out_specs=(P("tok", "mdl"), P("tok", None, None, "mdl")),
        check_vma=False,
    )
```

```python
import functools
import math

import jax
import jax.numpy as jnp
from jax import lax
from jax.experimental import pallas as pl
from jax.experimental.pallas import tpu as pltpu
from jax.sharding import PartitionSpec as P

HDIM = 128
SEGS = 4
EPSILON = 1e-05
MASKED = -1e30
VMEM_BYTES = 48 * 1024 * 1024
LARGE_VMEM_BYTES = 60 * 1024 * 1024
SCALE = math.log2(math.e) / math.sqrt(HDIM)


def rms_norm(hidden, norm_gain):
    values = hidden.astype(jnp.float32)
    factor = lax.rsqrt(jnp.mean(values * values, axis=-1, keepdims=True) + EPSILON)
    return (values * factor * norm_gain).astype(jnp.bfloat16)


def route_gates(normed, router_weight, routes):
    logits = jnp.dot(normed.astype(jnp.float32), router_weight, precision=lax.Precision.HIGHEST)
    expert_ids = jnp.arange(logits.shape[1], dtype=jnp.int32)
    picked = routes[:, :, None] == expert_ids[None, None, :]
    chosen = jnp.sum(jnp.where(picked, logits[:, None, :], jnp.float32(0.0)), axis=-1)
    gates = jax.nn.softmax(chosen, axis=-1)
    return jnp.sum(jnp.where(picked, gates[:, :, None], jnp.float32(0.0)), axis=1)


def params():
    return pltpu.CompilerParams(
        dimension_semantics=("arbitrary",), vmem_limit_bytes=VMEM_BYTES
    )


def kv_kernel(x_ref, w_ref, out_ref):
    depth = w_ref.shape[0] * w_ref.shape[2]
    w = w_ref[:, 0].reshape(depth, w_ref.shape[3])
    out_ref[0] = jnp.dot(x_ref[...], w, preferred_element_type=jnp.float32).astype(jnp.bfloat16)


def project_kv(normed, weight):
    shards, kinds, rows, cols = weight.shape
    tokens, width = normed.shape
    return pl.pallas_call(
        kv_kernel,
        grid=(kinds,),
        in_specs=[
            pl.BlockSpec((tokens, width), lambda c: (0, 0)),
            pl.BlockSpec((shards, 1, rows, cols), lambda c: (0, c, 0, 0)),
        ],
        out_specs=pl.BlockSpec((1, tokens, cols), lambda c: (c, 0, 0)),
        out_shape=jax.ShapeDtypeStruct((kinds, tokens, cols), jnp.bfloat16),
        compiler_params=params(),
        cost_estimate=pl.CostEstimate(
            flops=2 * kinds * tokens * width * cols,
            bytes_accessed=2 * (weight.size + normed.size + kinds * tokens * cols),
            transcendentals=0,
        ),
        name="project_kv",
    )(normed, weight)


def query_kernel(x_ref, routes_ref, w_ref, out_ref):
    expert = pl.program_id(0)
    depth = w_ref.shape[0] * w_ref.shape[2]
    w = w_ref[:, 0].reshape(depth, w_ref.shape[3])
    y = jnp.dot(x_ref[...], w, preferred_element_type=jnp.float32).astype(jnp.bfloat16)

    @pl.when(expert == 0)
    def _():
        out_ref[...] = jnp.zeros_like(out_ref)

    for slot in range(out_ref.shape[0]):
        mine = routes_ref[:, slot : slot + 1] == expert
        out_ref[slot] = jnp.where(mine, y, out_ref[slot])


def project_queries(normed, routes, weight):
    shards, experts, rows, cols = weight.shape
    tokens, width = normed.shape
    slots = routes.shape[1]
    return pl.pallas_call(
        query_kernel,
        grid=(experts,),
        in_specs=[
            pl.BlockSpec((tokens, width), lambda e: (0, 0)),
            pl.BlockSpec((tokens, slots), lambda e: (0, 0)),
            pl.BlockSpec((shards, 1, rows, cols), lambda e: (0, e, 0, 0)),
        ],
        out_specs=pl.BlockSpec((slots, tokens, cols), lambda e: (0, 0, 0)),
        out_shape=jax.ShapeDtypeStruct((slots, tokens, cols), jnp.bfloat16),
        compiler_params=params(),
        cost_estimate=pl.CostEstimate(
            flops=2 * experts * tokens * width * cols,
            bytes_accessed=2 * (weight.size + normed.size + slots * tokens * cols),
            transcendentals=0,
        ),
        name="project_queries",
    )(normed, routes, weight)


def attention_kernel(bounds_ref, q_ref, lower_ref, kv_ref, out_ref, *, block_k, heads, tile):
    pos_first = bounds_ref[0]
    step = pl.program_id(1)
    first = pos_first + step * tile
    low = bounds_ref[1 + 2 * step]
    high = bounds_ref[2 + 2 * step]
    slots = q_ref.shape[0]
    columns = slots * tile
    per_shard = kv_ref.shape[2] // block_k
    begin = low // block_k
    end = (first + tile - 1) // block_k + 1
    q_pos = first + lax.broadcasted_iota(jnp.int32, (1, columns), 1) % tile
    lower = jnp.concatenate([lower_ref[0]] * slots, axis=1)
    queries = [
        q_ref[:, :, h * HDIM : (h + 1) * HDIM].reshape(columns, HDIM) for h in range(heads)
    ]

    def body(block, carry, masked):
        shard = block // per_shard
        rows = pl.ds((block % per_shard) * block_k, block_k)
        if masked:
            k_pos = block * block_k + lax.broadcasted_iota(jnp.int32, (block_k, columns), 0)
            allowed = (k_pos >= lower) & (k_pos <= q_pos)
        result = []
        for h in range(heads):
            peak, total, accum = carry[h]
            span = slice(h * HDIM, (h + 1) * HDIM)
            keys = kv_ref[shard, 0, rows, span]
            values = kv_ref[shard, 1, rows, span]
            scores = lax.dot_general(
                keys, queries[h], (((1,), (1,)), ((), ())), preferred_element_type=jnp.float32
            ) * SCALE
            if masked:
                scores = jnp.where(allowed, scores, MASKED)
            new_peak = jnp.maximum(peak, jnp.max(scores, axis=0, keepdims=True))
            expon = jnp.exp2(scores - new_peak)
            if masked:
                expon = jnp.where(allowed, expon, 0.0)
            shrink = jnp.exp2(peak - new_peak)
            total = total * shrink + jnp.sum(expon, axis=0, keepdims=True)
            accum = accum * shrink + lax.dot_general(
                values,
                expon.astype(jnp.bfloat16),
                (((0,), (0,)), ((), ())),
                preferred_element_type=jnp.float32,
            )
            result.append((new_peak, total, accum))
        return tuple(result)

    state = tuple(
        (
            jnp.full((1, columns), MASKED, jnp.float32),
            jnp.zeros((1, columns), jnp.float32),
            jnp.zeros((HDIM, columns), jnp.float32),
        )
        for _ in range(heads)
    )
    inner = jnp.maximum((first + 1) // block_k, begin)
    clear = jnp.clip((high + block_k - 1) // block_k, begin, inner)
    state = lax.fori_loop(begin, clear, functools.partial(body, masked=True), state)
    state = lax.fori_loop(clear, inner, functools.partial(body, masked=False), state)
    state = lax.fori_loop(inner, end, functools.partial(body, masked=True), state)
    for h in range(heads):
        _, total, accum = state[h]
        rows = (accum / total).T.astype(jnp.bfloat16)
        out_ref[:, :, h * HDIM : (h + 1) * HDIM] = rows.reshape(slots, tile, HDIM)


def attend(queries, lower, key_values, first):
    slots, tokens, cols = queries.shape
    shards, kinds, rows, _ = key_values.shape
    heads = math.gcd(cols // HDIM, 2)
    tile = math.gcd(tokens, 256)
    block_k = math.gcd(rows, 512)
    by_tile = lower.reshape(tokens // tile, tile)
    bounds = jnp.concatenate(
        [first[None], jnp.stack([by_tile[:, 0], by_tile[:, -1]], axis=1).reshape(-1)]
    ).astype(jnp.int32)
    return pl.pallas_call(
        functools.partial(attention_kernel, block_k=block_k, heads=heads, tile=tile),
        grid=(cols // (heads * HDIM), tokens // tile),
        in_specs=[
            pl.BlockSpec(memory_space=pltpu.SMEM),
            pl.BlockSpec((slots, tile, heads * HDIM), lambda g, t: (0, t, g)),
            pl.BlockSpec((1, 1, tile), lambda g, t: (t, 0, 0)),
            pl.BlockSpec((shards, kinds, rows, heads * HDIM), lambda g, t: (0, 0, 0, g)),
        ],
        out_specs=pl.BlockSpec((slots, tile, heads * HDIM), lambda g, t: (0, t, g)),
        out_shape=jax.ShapeDtypeStruct((slots, tokens, cols), jnp.bfloat16),
        compiler_params=pltpu.CompilerParams(
            dimension_semantics=("arbitrary", "arbitrary"), vmem_limit_bytes=VMEM_BYTES
        ),
        cost_estimate=pl.CostEstimate(
            flops=4 * slots * tokens * cols * 2048,
            bytes_accessed=2 * (queries.size * 2 + key_values.size),
            transcendentals=slots * tokens * (cols // HDIM) * 2048,
        ),
        name="attend",
    )(bounds, queries, by_tile[:, None, :], key_values)


def out_kernel(x_ref, routes_ref, gates_ref, w_ref, out_ref, picked):
    experts = w_ref.shape[1]

    @pl.when(pl.program_id(0) == 0)
    def _():
        for e in range(experts):
            rows = jnp.zeros_like(x_ref[0])
            for slot in range(x_ref.shape[0]):
                rows = jnp.where(routes_ref[:, slot : slot + 1] == e, x_ref[slot], rows)
            picked[e] = rows

    total = jnp.zeros(out_ref.shape[1:], jnp.float32)
    for e in range(experts):
        term = jnp.dot(picked[e], w_ref[0, e], preferred_element_type=jnp.float32)
        total = total + gates_ref[:, e : e + 1] * term
    out_ref[0] = total.astype(jnp.bfloat16)


def project_out(attended, routes, gates, weight, parts):
    shards, experts, rows, cols = weight.shape
    slots, tokens, _ = attended.shape
    span = shards * cols // parts
    per = span // cols
    return pl.pallas_call(
        out_kernel,
        grid=(shards,),
        in_specs=[
            pl.BlockSpec((slots, tokens, rows), lambda i: (0, 0, 0)),
            pl.BlockSpec((tokens, slots), lambda i: (0, 0)),
            pl.BlockSpec((tokens, experts), lambda i: (0, 0)),
            pl.BlockSpec((1, experts, rows, cols), lambda i: (i, 0, 0, 0)),
        ],
        out_specs=pl.BlockSpec((1, tokens, cols), lambda i: (i // per, 0, i % per)),
        out_shape=jax.ShapeDtypeStruct((parts, tokens, span), jnp.bfloat16),
        scratch_shapes=[pltpu.VMEM((experts, tokens, rows), jnp.bfloat16)],
        compiler_params=params(),
        cost_estimate=pl.CostEstimate(
            flops=2 * experts * tokens * rows * shards * cols,
            bytes_accessed=2 * (weight.size + attended.size + tokens * shards * cols),
            transcendentals=0,
        ),
        name="project_out",
    )(attended, routes, gates, weight)


class TokRing:
    def __init__(self, order, send_sem, recv_sem, local_sem, lag, staged=False):
        self.lag, self.staged = lag, staged
        me = lax.axis_index("tok")
        core, col, row = me % 2, (me // 2) % 2, me // 4
        to_core, to_col, to_row = 1 - 2 * core, 2 - 4 * col, 4 - 8 * row
        self.me, self.to_core = me, to_core
        self.mate, self.side, self.over = me + to_core, me + to_col, me + to_row
        self.across = me + to_col + to_row
        self.order = order
        self.send_sem, self.recv_sem, self.local_sem = send_sem, recv_sem, local_sem

    def greet(self, along_mdl=()):
        barrier = pltpu.get_barrier_semaphore()
        for other in along_mdl:
            pl.semaphore_signal(
                barrier, inc=1, device_id={"mdl": other}, device_id_type=pl.DeviceIdType.MESH
            )
        for other in (self.mate, self.side, self.over):
            pl.semaphore_signal(
                barrier, inc=1, device_id={"tok": other}, device_id_type=pl.DeviceIdType.MESH
            )
        pl.semaphore_wait(barrier, 3 + len(along_mdl))

    def half(self, ref, part):
        rows = ref.shape[0] // 2
        return ref.at[pl.ds(part * rows, rows)]

    def copy(self, k, way, src, dst, other):
        return pltpu.make_async_remote_copy(
            src_ref=src,
            dst_ref=dst,
            send_sem=self.send_sem.at[k, way],
            recv_sem=self.recv_sem.at[k, way],
            device_id={"tok": other},
            device_id_type=pl.DeviceIdType.MESH,
        )

    def send(self, k, way):
        own, slot = self.order[k]
        if way < 3:
            own = slot(self.me) if self.staged else own
            return self.copy(k, way, own, slot(self.me), (self.mate, self.side, self.over)[way])
        place, other = [
            lambda: (self.half(slot(self.over), 0), self.side),
            lambda: (self.half(slot(self.side), 1), self.over),
            lambda: (slot(self.side), self.mate),
            lambda: (slot(self.over), self.mate),
            lambda: (slot(self.across), self.mate),
        ][way - 3]()
        return self.copy(k, way, place, place, other)

    def arrival(self, k, way):
        slot = self.order[k][1]
        place = [
            lambda: slot(self.mate),
            lambda: slot(self.side),
            lambda: slot(self.over),
            lambda: self.half(slot(self.across), 0),
            lambda: self.half(slot(self.across), 1),
            lambda: slot(self.side + self.to_core),
            lambda: slot(self.over + self.to_core),
            lambda: slot(self.across + self.to_core),
        ][way]()
        return self.copy(k, way, place, place, self.mate)

    def keep(self, k):
        own, slot = self.order[k]
        return pltpu.make_async_copy(own, slot(self.me), self.local_sem.at[k])

    def begin(self, k):
        if self.staged:
            self.keep(k).wait()
        for way in (1, 2, 0):
            self.send(k, way).start()
        if not self.staged:
            self.keep(k).start()

    def forward(self, k):
        self.arrival(k, 1).wait_recv()
        self.send(k, 4).start()
        self.send(k, 5).start()
        self.arrival(k, 2).wait_recv()
        self.send(k, 3).start()
        self.send(k, 6).start()

    def share(self, k):
        self.arrival(k, 3).wait_recv()
        self.arrival(k, 4).wait_recv()
        self.send(k, 7).start()

    def complete(self, k):
        for way in (0, 5, 6, 7):
            self.arrival(k, way).wait_recv()
        if not self.staged:
            self.keep(k).wait()

    def step(self, k, finish=None):
        count = len(self.order)
        if k < count:
            self.begin(k)
        j = k - self.lag
        if 0 <= j < count:
            self.forward(j)
        if 0 <= j - 1 < count:
            self.share(j - 1)
        if 0 <= j - 2 < count:
            self.complete(j - 2)
            if finish is not None:
                finish(j - 2)

    def drain(self):
        for k in range(len(self.order)):
            for way in range(8):
                self.send(k, way).wait_send()


def gather_kernel(
    hidden_ref,
    gain_ref,
    router_ref,
    routes_ref,
    table_ref,
    kvw_ref,
    qw_ref,
    q_ref,
    gates_ref,
    tables_ref,
    gathered_ref,
    x_ref,
    weights,
    own_kv,
    send_sem,
    recv_sem,
    local_sem,
):
    kinds, experts = kvw_ref.shape[0], qw_ref.shape[0]

    def weight(c):
        own = kvw_ref.at[c] if c < kinds else qw_ref.at[c - kinds]
        return (own, lambda shard: weights.at[c, shard])

    def pair(c):
        return (own_kv.at[c], lambda shard: gathered_ref.at[shard, c])

    table = (table_ref, lambda shard: tables_ref.at[shard])
    early = min(2, experts)
    labels = [("w", c) for c in range(kinds)] + [("table", 0)]
    labels += [("w", c) for c in range(kinds, kinds + early)]
    labels += [("kv", c) for c in range(kinds)]
    labels += [("w", c) for c in range(kinds + early, kinds + experts)]
    order = [table if n == "table" else weight(c) if n == "w" else pair(c) for n, c in labels]
    ring = TokRing(order, send_sem, recv_sem, local_sem, 1)
    ring.greet()

    def normalise():
        values = hidden_ref[...].astype(jnp.float32)
        factor = lax.rsqrt(jnp.mean(values * values, axis=-1, keepdims=True) + EPSILON)
        x_ref[...] = (values * factor * gain_ref[...]).astype(jnp.bfloat16)

    def gate():
        logits = lax.dot_general(
            x_ref[...].astype(jnp.float32),
            router_ref[...],
            (((1,), (1,)), ((), ())),
            precision=lax.Precision.HIGHEST,
            preferred_element_type=jnp.float32,
        )
        ids = lax.broadcasted_iota(jnp.int32, logits.shape, 1)
        picked = [routes_ref[:, s : s + 1] == ids for s in range(routes_ref.shape[1])]
        chosen = [jnp.sum(jnp.where(p, logits, 0.0), axis=1, keepdims=True) for p in picked]
        top = functools.reduce(jnp.maximum, chosen)
        expon = [jnp.exp(c - top) for c in chosen]
        total = functools.reduce(jnp.add, expon)
        result = jnp.zeros_like(logits)
        for p, e in zip(picked, expon):
            result = jnp.where(p, e / total, result)
        gates_ref[...] = result

    def finish(k):
        kind, c = labels[k]
        if kind != "w":
            return
        depth = weights.shape[1] * weights.shape[2]
        w = weights[c].reshape(depth, weights.shape[3])
        y = jnp.dot(x_ref[...], w, preferred_element_type=jnp.float32).astype(jnp.bfloat16)
        if c < kinds:
            own_kv[c] = y
            return
        expert = c - kinds
        for s in range(q_ref.shape[0]):
            mine = routes_ref[:, s : s + 1] == expert
            before = jnp.zeros_like(y) if expert == 0 else q_ref[s]
            q_ref[s] = jnp.where(mine, y, before)

    for k in range(len(order) + 3):
        ring.step(k, finish)
        if k == 0:
            normalise()
        if k == 6:
            gate()
    ring.drain()


def gather_project(hidden, norm_gain, router_weight, routes, table, kv_weight, query_weight, shards):
    tokens, width = hidden.shape
    kinds, rows, cols = kv_weight.shape
    experts = query_weight.shape[0]
    slots = routes.shape[1]
    chunks = 2 * kinds + experts + 1
    vmem = pl.BlockSpec(memory_space=pltpu.VMEM)
    anywhere = pl.BlockSpec(memory_space=pl.ANY)
    return pl.pallas_call(
        gather_kernel,
        in_specs=[vmem, vmem, vmem, vmem, vmem, anywhere, anywhere],
        out_specs=[vmem, vmem, vmem, anywhere],
        out_shape=[
            jax.ShapeDtypeStruct((slots, tokens, cols), jnp.bfloat16),
            jax.ShapeDtypeStruct((tokens, experts), jnp.float32),
            jax.ShapeDtypeStruct((shards,) + table.shape, jnp.int32),
            jax.ShapeDtypeStruct((shards, kinds, tokens, cols), jnp.bfloat16),
        ],
        scratch_shapes=[
            pltpu.VMEM((tokens, width), jnp.bfloat16),
            pltpu.VMEM((kinds + experts, shards, rows, cols), jnp.bfloat16),
            pltpu.VMEM((kinds, tokens, cols), jnp.bfloat16),
            pltpu.SemaphoreType.DMA((chunks, 8)),
            pltpu.SemaphoreType.DMA((chunks, 8)),
            pltpu.SemaphoreType.DMA((chunks,)),
        ],
        compiler_params=pltpu.CompilerParams(
            collective_id=1, has_side_effects=True, vmem_limit_bytes=LARGE_VMEM_BYTES
        ),
        cost_estimate=pl.CostEstimate(
            flops=2 * (kinds + experts) * tokens * width * cols * 10,
            bytes_accessed=200 * 1024 * 1024,
            transcendentals=0,
        ),
        name="gather_project",
    )(hidden, norm_gain[None, :], router_weight.T, routes, table, kv_weight, query_weight)


def attend_out_kernel(
    q_ref,
    lower_ref,
    routes_ref,
    gates_ref,
    residual_ref,
    kv_ref,
    ow_ref,
    out_ref,
    held,
    attended,
    weights,
    picked,
    own,
    near,
    far,
    load_sem,
    send_sem,
    recv_sem,
    local_sem,
    sum_send_sem,
    sum_recv_sem,
    *,
    tile,
    block_k,
    heads,
    most,
):
    experts = ow_ref.shape[0]
    slots, tokens, cols = q_ref.shape
    shards = kv_ref.shape[0]
    halves, lanes = weights.shape[0], weights.shape[4]
    per = shards // 4
    mdl = lax.axis_index("mdl")
    low, high = mdl % 2, mdl // 2
    near_id, far_id = mdl + 1 - 2 * low, mdl + 2 - 4 * high
    targets = [near_id + 2 - 4 * high, near_id, far_id, mdl]
    load = pltpu.make_async_copy(kv_ref, held, load_sem)

    def chunk(h, n):
        pick = pl.ds(n * batch, batch)
        own = ow_ref.at[pick, :, pl.ds(h * lanes, lanes)]
        return (own, lambda shard: weights.at[h, shard, pick])

    batch = 2
    chunks = experts // batch
    order = [chunk(h, n) for h in range(halves) for n in range(chunks)]
    ring = TokRing(order, send_sem, recv_sem, local_sem, 2, staged=True)
    for n in range(len(order)):
        ring.keep(n).start()
    load.start()
    ring.greet((near_id, far_id))
    ring.step(0)
    ring.step(1)
    columns = slots * tile
    per_shard = tokens // block_k

    def attend_tile(group, step):
        first = ring.me * tokens + step * tile
        begin = jnp.maximum(first + 1 - most, 0) // block_k
        inner = (first + 1) // block_k
        end = (first + tile - 1) // block_k + 1
        lower = jnp.concatenate([lower_ref[step]] * slots, axis=1)
        q_pos = first + lax.broadcasted_iota(jnp.int32, (1, columns), 1) % tile
        spans = [slice((group * heads + h) * HDIM, (group * heads + h + 1) * HDIM) for h in range(heads)]
        rows_q = slice(step * tile, (step + 1) * tile)
        queries = [q_ref[:, rows_q, span].reshape(columns, HDIM) for span in spans]

        def body(block, carry, causal):
            shard = block // per_shard
            rows = pl.ds((block % per_shard) * block_k, block_k)
            k_pos = block * block_k + lax.broadcasted_iota(jnp.int32, (block_k, columns), 0)
            allowed = k_pos >= lower
            if causal:
                allowed = allowed & (k_pos <= q_pos)
            result = []
            for h in range(heads):
                peak, total, accum = carry[h]
                keys = held[shard, 0, rows, spans[h]]
                values = held[shard, 1, rows, spans[h]]
                scores = lax.dot_general(
                    keys, queries[h], (((1,), (1,)), ((), ())), preferred_element_type=jnp.float32
                ) * SCALE
                scores = jnp.where(allowed, scores, MASKED)
                new_peak = jnp.maximum(peak, jnp.max(scores, axis=0, keepdims=True))
                expon = jnp.exp2(scores - new_peak)
                shrink = jnp.exp2(peak - new_peak)
                total = total * shrink + jnp.sum(expon, axis=0, keepdims=True)
                accum = accum * shrink + lax.dot_general(
                    values,
                    expon.astype(jnp.bfloat16),
                    (((0,), (0,)), ((), ())),
                    preferred_element_type=jnp.float32,
                )
                result.append((new_peak, total, accum))
            return tuple(result)

        state = tuple(
            (
                jnp.full((1, columns), MASKED, jnp.float32),
                jnp.zeros((1, columns), jnp.float32),
                jnp.zeros((HDIM, columns), jnp.float32),
            )
            for _ in range(heads)
        )
        state = lax.fori_loop(begin, inner, functools.partial(body, causal=False), state)
        state = lax.fori_loop(inner, end, functools.partial(body, causal=True), state)
        for h in range(heads):
            _, total, accum = state[h]
            part = (accum / total).T.astype(jnp.bfloat16)
            attended[:, rows_q, spans[h]] = part.reshape(slots, tile, HDIM)

    def sum_copy(way, src, dst, other):
        return pltpu.make_async_remote_copy(
            src_ref=src,
            dst_ref=dst,
            send_sem=sum_send_sem.at[way],
            recv_sem=sum_recv_sem.at[way],
            device_id={"mdl": other},
            device_id_type=pl.DeviceIdType.MESH,
        )

    def near_copy(h, n):
        return sum_copy(3 * h + n, own.at[h, n], near.at[h, n], near_id)

    def far_copy(h):
        return sum_copy(3 * h + 2, own.at[h, 2], far.at[h], far_id)

    def block(h, n):
        total = jnp.zeros(own.shape[2:], jnp.float32)
        for e in range(experts):
            w = jnp.concatenate([weights[h, targets[n] * per + s, e] for s in range(per)], axis=1)
            term = jnp.dot(picked[e], w, preferred_element_type=jnp.float32)
            total = total + gates_ref[:, e : e + 1] * term
        own[h, n] = total.astype(jnp.bfloat16)

    def pass_on(h):
        near_copy(h, 0).wait_recv()
        both = own[h, 2].astype(jnp.float32) + near[h, 0].astype(jnp.float32)
        own[h, 2] = both.astype(jnp.bfloat16)
        far_copy(h).start()

    def close(h):
        near_copy(h, 1).wait_recv()
        far_copy(h).wait_recv()
        mine = own[h, 3].astype(jnp.float32) + near[h, 1].astype(jnp.float32)
        mine = mine + far[h].astype(jnp.float32)
        for s in range(per):
            at = slice((s * halves + h) * lanes, (s * halves + h + 1) * lanes)
            part = residual_ref[:, at].astype(jnp.float32) + mine[:, s * lanes : (s + 1) * lanes]
            out_ref[:, at] = part.astype(jnp.bfloat16)

    load.wait()
    k = 2
    for group in range(cols // (heads * HDIM)):
        for step in range(tokens // tile):
            attend_tile(group, step)
            ring.step(k)
            k += 1
    for e in range(experts):
        rows = jnp.zeros_like(attended[0])
        for s in range(slots):
            rows = jnp.where(routes_ref[:, s : s + 1] == e, attended[s], rows)
        picked[e] = rows
    last = len(order) + ring.lag + 2
    for h in range(halves):
        ready = (h + 1) * chunks + ring.lag + 2
        for rest in range(k, ready):
            ring.step(rest)
        k = max(k, ready)
        for n in range(4):
            block(h, n)
            if n < 2:
                near_copy(h, n).start()
            if h + 1 < halves and k < last - 2:
                ring.step(k)
                k += 1
        pass_on(h)
    for h in range(halves):
        close(h)
    ring.drain()
    for h in range(halves):
        near_copy(h, 0).wait_send()
        near_copy(h, 1).wait_send()
        far_copy(h).wait_send()


def attend_out(queries, lower, routes, gates, residual, key_values, out_weight, most):
    slots, tokens, cols = queries.shape
    shards = key_values.shape[0]
    experts, rows, out_cols = out_weight.shape
    heads = math.gcd(cols // HDIM, 2)
    tile = math.gcd(tokens, 256)
    halves = 2
    lanes = out_cols // halves
    width = shards // 4 * lanes
    vmem = pl.BlockSpec(memory_space=pltpu.VMEM)
    anywhere = pl.BlockSpec(memory_space=pl.ANY)
    return pl.pallas_call(
        functools.partial(
            attend_out_kernel, tile=tile, block_k=math.gcd(tokens, 512), heads=heads, most=most
        ),
        in_specs=[vmem] * 5 + [anywhere] * 2,
        out_specs=vmem,
        out_shape=jax.ShapeDtypeStruct(residual.shape, jnp.bfloat16),
        scratch_shapes=[
            pltpu.VMEM(key_values.shape, jnp.bfloat16),
            pltpu.VMEM((slots, tokens, cols), jnp.bfloat16),
            pltpu.VMEM((halves, shards, experts, rows, lanes), jnp.bfloat16),
            pltpu.VMEM((experts, tokens, rows), jnp.bfloat16),
            pltpu.VMEM((halves, 4, tokens, width), jnp.bfloat16),
            pltpu.VMEM((halves, 2, tokens, width), jnp.bfloat16),
            pltpu.VMEM((halves, tokens, width), jnp.bfloat16),
            pltpu.SemaphoreType.DMA,
            pltpu.SemaphoreType.DMA((halves * experts, 8)),
            pltpu.SemaphoreType.DMA((halves * experts, 8)),
            pltpu.SemaphoreType.DMA((halves * experts,)),
            pltpu.SemaphoreType.DMA((3 * halves,)),
            pltpu.SemaphoreType.DMA((3 * halves,)),
        ],
        compiler_params=pltpu.CompilerParams(
            collective_id=3, has_side_effects=True, vmem_limit_bytes=LARGE_VMEM_BYTES
        ),
        cost_estimate=pl.CostEstimate(
            flops=4 * slots * tokens * cols * most * 10,
            bytes_accessed=2 * (queries.size * 2 + key_values.size + 2 * shards * out_weight.size),
            transcendentals=slots * tokens * (cols // HDIM) * most,
        ),
        name="attend_out",
    )(
        queries,
        lower.reshape(tokens // tile, 1, tile),
        routes,
        gates,
        residual,
        key_values,
        out_weight,
    )


def local(
    hidden,
    segment_ids,
    routes,
    norm_gain,
    router_weight,
    query_weight,
    kv_weight,
    out_weight,
    page_table,
):
    tok_dev, width = hidden.shape
    head_cols = query_weight.shape[2]
    shards = lax.axis_size("tok")
    parts = lax.axis_size("mdl")
    tok_row = lax.axis_index("tok")
    pages_here = page_table.shape[0]
    page_rows = tok_dev // pages_here

    own_kernels = shards == 8 and parts == 4
    if own_kernels:
        padded = jnp.zeros((16, 128), jnp.int32).at[0, :pages_here].set(page_table)
        queries, gates, tables, key_values = gather_project(
            hidden, norm_gain, router_weight, routes, padded, kv_weight, query_weight, shards
        )
        table = tables[:, 0, :pages_here].reshape(-1)
    else:
        table = lax.all_gather(page_table, "tok", axis=0, tiled=True)
        normed = rms_norm(hidden, norm_gain)
        gates = route_gates(normed, router_weight, routes)
        out_full = lax.all_gather(out_weight, "tok", axis=0)
        kv_full = lax.all_gather(kv_weight, "tok", axis=0)
        key_values = lax.all_gather(project_kv(normed, kv_full), "tok", axis=0)
        query_full = lax.all_gather(query_weight, "tok", axis=0)
        queries = project_queries(normed, routes, query_full)

    here = tok_row * pages_here + jnp.arange(pages_here, dtype=jnp.int32)
    logical = jnp.arange(table.shape[0], dtype=jnp.int32)
    source = jnp.sum(jnp.where(table[None, :] == here[:, None], logical[None, :], 0), axis=1)
    paged = key_values.reshape(shards, 2, pages_here, page_rows, head_cols)
    cache = paged[source // pages_here, :, source % pages_here].transpose(0, 2, 1, 3)

    prompt_ids = jnp.arange(SEGS, dtype=jnp.int32)
    seg_first = jnp.sum((segment_ids[:, None] < prompt_ids[None, :]).astype(jnp.int32), axis=0)
    first = (tok_row * tok_dev).astype(jnp.int32)
    own_seg = lax.dynamic_slice_in_dim(segment_ids, first, tok_dev, 0)
    lower = jnp.sum(
        jnp.where(own_seg[:, None] == prompt_ids[None, :], seg_first[None, :], 0), axis=1
    )

    span = width // parts
    residual = lax.dynamic_slice_in_dim(hidden, lax.axis_index("mdl") * span, span, 1)
    if own_kernels:
        most = segment_ids.shape[0] // 2
        args = (queries, lower, routes, gates, residual, key_values, out_weight, most)
        return (attend_out(*args), cache)
    attended = attend(queries, lower, key_values, first)
    partial_sums = project_out(attended, routes, gates, out_full, parts)
    mine = lax.psum_scatter(partial_sums, "mdl", scatter_dimension=0, tiled=False)
    output = (residual.astype(jnp.float32) + mine.astype(jnp.float32)).astype(jnp.bfloat16)
    return (output, cache)


def solution(mesh):
    placed = (
        P("tok", None),
        P(),
        P("tok", None),
        P(),
        P(),
        P(None, "tok", "mdl"),
        P(None, "tok", "mdl"),
        P(None, "mdl", "tok"),
        P("tok"),
    )
    return jax.shard_map(
        local,
        mesh=mesh,
        in_specs=placed,
        out_specs=(P("tok", "mdl"), P("tok", None, None, "mdl")),
        check_vma=False,
    )
```
